512 devices in a mesh: pairs: 64 (over z, y_hi, x), dims: 8 (over y_lo, core).
Axes of the slice: x: 4, y: 8 (y_hi: 2, y_lo: 4; y = y_hi * 4 + y_lo), z: 8, core: 2. Of those that a mesh axis runs over, the one named last changes fastest.
Arguments:
- first_view: bfloat16 [8192, 4096], P('pairs', 'dims'), may hold values from -40 to 40
- second_view: bfloat16 [8192, 4096], P('pairs', 'dims'), may hold values from -40 to 40
- weight: bfloat16 [4096, 4096], P(None, 'dims'), may hold values from -0.09375 to 0.09375
- pre_act: bfloat16 [8192, 4096], P('pairs', 'dims'), may hold values from -6 to 6
Outputs:
- view_grad: bfloat16 [8192, 4096], P('pairs', 'dims')
- pre_grad: bfloat16 [8192, 4096], P('pairs', 'dims')
The draws below stay inside these ranges and needn't reach their ends.
All inputs are finite; a program needn't handle non-finite values.
Results may differ from the reference program's by a relative error of at most 0.017.
Values may be sent and summed in bfloat16 or wider, within the bound.
A program may use at most 64 MiB of HBM per device.

```python
import math
import jax
import jax.numpy as jnp
from jax import lax

D = 4096
DIN = 4096
TOK_DEV = 128
TOKENS = 8192
N_DIMS = 8


def shared_view(key, offset_scale):
    subkeys = jax.random.split(key, 3)
    positions = jnp.arange(TOKENS, dtype=jnp.float32)
    row_scale = 10.0 ** (positions / (TOKENS - 1) - 0.5)
    col_scale = jnp.exp(jax.random.uniform(subkeys[1], (D,), jnp.float32, math.log(0.1), math.log(2.0)))
    offsets = jax.random.normal(subkeys[2], (D,), jnp.float32) * offset_scale
    gauss = jax.random.normal(subkeys[0], (TOKENS, D), jnp.float32)
    scales = row_scale[:, None] * col_scale[None, :]
    values = offsets[None, :] + gauss * scales
    return (values, scales)


def draw_first_view(key, part):
    values, scales = shared_view(key, 2.0)
    return jnp.clip(values, -40.0, 40.0).astype(jnp.bfloat16)


def draw_second_view(key, part):
    values, scales = shared_view(key, 2.0)
    key = jax.random.fold_in(key, 5)
    offset_noise = jax.random.normal(key, (TOKENS, D), jnp.float32) * 0.3 * scales
    return jnp.clip(values + offset_noise, -40.0, 40.0).astype(jnp.bfloat16)


def steps_of(key, dims, pieces, smallest, largest):
    def one(position, blocks):
        draws = jax.random.uniform(jax.random.fold_in(jax.random.fold_in(key, 6), position), (blocks,), jnp.float32, smallest / len(pieces), largest / len(pieces))
        return jnp.repeat(jnp.exp(draws), dims[position] // blocks).reshape((-1,) + (1,) * (len(dims) - position - 1))

    gain = one(*pieces[0])
    for cut in pieces[1:]:
        gain = gain * one(*cut)
    return gain


def noise(stream_key, shape, scale, bound, pieces=(), kind=jnp.bfloat16):
    entries = scale * jax.random.normal(stream_key, shape, jnp.float32)
    if pieces:
        entries = entries * steps_of(stream_key, shape, pieces, -0.22, 0.18)
    return jnp.clip(entries, -bound, bound).astype(kind)


def setup_inputs(seed: int = 0) -> dict:
    key_of = jax.random.split(jax.random.key(seed), 5)
    return {
        "first_view": draw_first_view(jax.random.fold_in(key_of[4], 71), 0),
        "second_view": draw_second_view(jax.random.fold_in(key_of[4], 71), 0),
        "weight": noise(key_of[2], (DIN, D), DIN ** -0.5, 0.09375, ((1, 8),)),
        "pre_act": noise(key_of[3], (TOKENS, DIN), 1.0, 6.0, ((0, 64), (1, 8))),
    }


inv_weight = 25.0
var_weight = 25.0
cov_weight = 1.0
var_eps = 1e-05
loss_share = 32.0

def reference(first_view, second_view, weight, pre_act):
    values = first_view.astype(jnp.float32)
    column_mean = lax.optimization_barrier(jnp.sum(values, axis=0)) / TOKENS
    centered = values - column_mean
    packed = centered.astype(jnp.bfloat16)
    variance = lax.optimization_barrier(jnp.sum(centered * centered, axis=0)) / (TOKENS - 1)
    deviation = jnp.sqrt(variance + var_eps)
    width = D // N_DIMS
    row_blocks = packed.reshape(TOKENS // TOK_DEV, TOK_DEV, D)

    def block_product(block_rows):
        gram = jnp.zeros((TOK_DEV, TOKENS), jnp.float32)
        for block_index in range(N_DIMS):
            lower = block_index * width
            term = lax.dot_general(block_rows[:, lower:lower + width], packed[:, lower:lower + width], (((1,), (1,)), ((), ())), preferred_element_type=jnp.float32)
            gram = gram + lax.optimization_barrier(term.astype(jnp.bfloat16)).astype(jnp.float32)
        return jnp.dot(gram.astype(jnp.bfloat16), packed, preferred_element_type=jnp.float32)
    cov_prod = lax.map(block_product, row_blocks).reshape(TOKENS, D)
    factor = TOKENS * D / loss_share
    invariance = 2.0 * inv_weight / (TOKENS * D) * (values - second_view.astype(jnp.float32))
    hinge = jnp.where(deviation < 1.0, 1.0, 0.0).astype(jnp.float32)
    spread_term = -var_weight / D * hinge * centered / ((TOKENS - 1) * deviation)
    cov_term = 4.0 * cov_weight / (D * (TOKENS - 1)) * (cov_prod / (TOKENS - 1) - centered * variance)
    view_grad = (factor * (invariance + spread_term + cov_term)).astype(jnp.bfloat16)
    back = lax.dot_general(view_grad, weight, (((1,), (1,)), ((), ())), preferred_element_type=jnp.float32)
    pre_grad = jnp.where(pre_act > 0, back, 0.0).astype(jnp.bfloat16)
    return (view_grad, pre_grad)
```

```python
import jax
import jax.numpy as jnp
from jax import lax
from jax.experimental import pallas as pl
from jax.experimental.pallas import tpu as pltpu
from jax.sharding import PartitionSpec as P

D = 4096
N = 8192
ROWS = 128
COLS = 512
UNIT = 64

inv_weight = 25.0
var_weight = 25.0
cov_weight = 1.0
var_eps = 1e-05
loss_share = 32.0

F32 = jnp.float32
BF16 = jnp.bfloat16
NT = (((1,), (1,)), ((), ()))
TN = (((0,), (0,)), ((), ()))


def kernel(
    fv, sv, w, pa, vg_out, pg_out,
    xj, xk, pj, pk, svb, wb, pab,
    own, st1, tot, st2, msq, st3,
    cf, rs_s, rs_r, yh_s, yh_r, call,
    cx_s, cx_r, db_s, db_r, bk_s, bk_r, keep,
    lsem,
    xj_ss, xj_rs, xk_ss, xk_rs,
    s1_ss, s1_rs, s2_ss, s2_rs, s3_ss, s3_rs,
    pk_ss, pk_rs, rsz_ss, rsz_rs, yh_ss, yh_rs, ag_ss, ag_rs,
    cx_ss, cx_rs, db_ss, db_rs, bk_ss, bk_rs,
):
    p = lax.axis_index("pairs")
    d = lax.axis_index("dims")
    z, yh, x = p // 8, (p // 4) % 2, p % 4
    yl, c = d // 2, d % 2

    def dev(z_, yh_, x_, yl_, c_):
        return (z_ * 8 + yh_ * 4 + x_, yl_ * 2 + c_)

    def to_x(r):
        return dev(z, yh, (x + r) % 4, yl, c)

    def to_k(r):
        return dev(z, yh, yl, (x + r) % 4, c)

    def from_k(r):
        return dev(z, yh, (yl + 4 - r) % 4, x, c)

    def to_yl(r):
        return dev(z, yh, x, (yl + r) % 4, c)

    def to_zy(r):
        return dev((z + r % 8) % 8, (yh + r // 8) % 2, x, yl, c)

    partner = dev(z, yh, x, yl, 1 - c)
    diagonal = x == yl

    def remote(src, dst, ss, rs, to):
        return pltpu.make_async_remote_copy(
            src_ref=src, dst_ref=dst, send_sem=ss, recv_sem=rs,
            device_id=to, device_id_type=pl.DeviceIdType.MESH)

    load_x = pltpu.make_async_copy(fv, xj.at[x], lsem.at[0])
    load_x.start()
    load_w = pltpu.make_async_copy(w, wb, lsem.at[1])
    load_s = pltpu.make_async_copy(sv, svb, lsem.at[2])
    load_p = pltpu.make_async_copy(pa, pab, lsem.at[3])
    load_k = pltpu.make_async_copy(fv, xk.at[x], lsem.at[4])

    barrier = pltpu.get_barrier_semaphore()

    def greet(to):
        pl.semaphore_signal(barrier, inc=1, device_id=to, device_id_type=pl.DeviceIdType.MESH)

    count = 0
    for r in range(1, 16):
        greet(to_zy(r))
        count += 1
    for r in range(1, 4):
        greet(to_x(r))
        greet(to_k(r))
        greet(from_k(r))
        greet(to_yl(r))
        count += 4
    greet(partner)
    count += 1

    @pl.when(jnp.logical_not(diagonal))
    def _():
        greet(to_k(0))
        greet(from_k(0))

    @pl.when(diagonal)
    def _():
        load_k.start()

    load_w.start()
    load_s.start()
    load_p.start()
    load_x.wait()
    own[...] = jnp.sum(xj[x].astype(F32), axis=0, keepdims=True)

    @pl.when(jnp.logical_not(diagonal))
    def _():
        pl.semaphore_wait(barrier, count + 2)

    @pl.when(diagonal)
    def _():
        pl.semaphore_wait(barrier, count)

    s1j = [remote(own, st1.at[0, r], s1_ss.at[0, r], s1_rs.at[0, r], to_x(r)) for r in range(1, 4)]
    s1k = [remote(own, st1.at[1, r], s1_ss.at[1, r], s1_rs.at[1, r], to_k(r)) for r in range(4)]
    gj = [remote(xj.at[x], xj.at[x], xj_ss.at[r], xj_rs.at[r], to_x(r)) for r in range(1, 4)]
    gk = [remote(xj.at[x], xk.at[x], xk_ss.at[r], xk_rs.at[r], to_k(r)) for r in range(4)]
    for cp in s1j + s1k[1:]:
        cp.start()

    @pl.when(jnp.logical_not(diagonal))
    def _():
        s1k[0].start()
        gk[0].start()

    for cp in gk[1:] + gj:
        cp.start()

    @pl.when(diagonal)
    def _():
        st1[1, 0] = own[...]

    for cp in s1j:
        cp.wait_recv()
    tot[0] = own[...] + st1[0, 1] + st1[0, 2] + st1[0, 3]

    @pl.when(jnp.logical_not(diagonal))
    def _():
        s1k[0].wait_recv()

    for cp in s1k[1:]:
        cp.wait_recv()
    tot[1] = st1[1, 0] + st1[1, 1] + st1[1, 2] + st1[1, 3]
    s2 = [remote(tot, st2.at[r], s2_ss.at[r], s2_rs.at[r], to_zy(r)) for r in range(1, 16)]
    for cp in s2:
        cp.start()
    for cp in s2:
        cp.wait_recv()
    mean = tot[...]
    for r in range(1, 16):
        mean = mean + st2[r]
    mean = mean / N
    mean_j, mean_k = mean[0], mean[1]

    for cp in gk[1:]:
        cp.wait_recv()

    @pl.when(jnp.logical_not(diagonal))
    def _():
        gk[0].wait_recv()

    @pl.when(diagonal)
    def _():
        load_k.wait()

    @pl.loop(0, 4)
    def _(b):
        pk[0, b] = (xk[b].astype(F32) - mean_k).astype(BF16)

    share = remote(pk.at[0], pk.at[1], pk_ss, pk_rs, partner)
    share.start()
    for cp in gj:
        cp.wait_recv()
    msq[...] = jnp.zeros_like(msq)

    @pl.loop(0, 4)
    def _(b):
        centered = xj[b].astype(F32) - mean_j
        pj[b] = centered.astype(BF16)
        msq[...] += jnp.sum(centered * centered, axis=0, keepdims=True)

    s3 = [remote(msq, st3.at[r], s3_ss.at[r], s3_rs.at[r], to_zy(r)) for r in range(1, 16)]

    def block(h):
        prod = lax.dot_general(
            pj[...].reshape(4 * ROWS, COLS), pk[h].reshape(4 * ROWS, COLS), TN,
            preferred_element_type=F32)
        cf[h] = prod.reshape(8, UNIT, COLS)

    block(0)
    share.wait_recv()
    block(1)

    def near(way):
        return dev((z + (1 if way == 0 else 7)) % 8, yh, x, yl, c)

    rs = {}
    for n in range(7):
        for way in range(2):
            h = (n + way) % 2
            k = 4 - (n + 1) // 2
            unit = (z + (k if way == 0 else 8 - k)) % 8
            val = cf[h, unit]
            if n >= 2:
                rs[n - 2, way].wait_recv()
                val = val + rs_r[way, n - 2].astype(F32)
            rs_s[way, n] = val.astype(BF16)
            rs[n, way] = remote(
                rs_s.at[way, n], rs_r.at[way, n], rsz_ss.at[way, n], rsz_rs.at[way, n], near(way))
            rs[n, way].start()
        if n == 1:
            for cp in s3:
                cp.start()
    swap = []
    for n in (5, 6):
        rs[n, 0].wait_recv()
        rs[n, 1].wait_recv()
    for h in range(2):
        mine = cf[h, z] + rs_r[0, 6 - h].astype(F32) + rs_r[1, 5 + h].astype(F32)
        cf[h, z] = mine
        yh_s[h] = mine.astype(BF16)
        cp = remote(yh_s.at[h], yh_r.at[h], yh_ss.at[h], yh_rs.at[h], to_zy(8))
        cp.start()
        swap.append(cp)
    for h in range(2):
        swap[h].wait_recv()
        call[h, z] = (cf[h, z] + yh_r[h].astype(F32)).astype(BF16)

    ag = {}
    for n in range(7):
        for way in range(2):
            h = (n + way) % 2
            o = n // 2
            unit = (z + (8 - o if way == 0 else o)) % 8
            if n >= 2:
                ag[n - 2, way].wait_recv()
            ag[n, way] = remote(
                call.at[h, unit], call.at[h, unit], ag_ss.at[way, n], ag_rs.at[way, n], near(way))
            ag[n, way].start()

    for cp in s3:
        cp.wait_recv()
    variance = msq[...]
    for r in range(1, 16):
        variance = variance + st3[r]
    variance = variance / (N - 1)
    deviation = jnp.sqrt(variance + var_eps)
    hinge = jnp.where(deviation < 1.0, 1.0, 0.0).astype(F32)
    for n in (5, 6):
        ag[n, 0].wait_recv()
        ag[n, 1].wait_recv()

    def product(b):
        out = lax.dot_general(
            pk[0, b], call[0].reshape(8 * UNIT, COLS), NT, preferred_element_type=F32)
        return out + lax.dot_general(
            pk[1, b], call[1].reshape(8 * UNIT, COLS), NT, preferred_element_type=F32)

    cx = []
    for r in (2, 1, 3):
        cx_s[r] = product((x + r) % 4).astype(BF16)
        cp = remote(cx_s.at[r], cx_r.at[r], cx_ss.at[r], cx_rs.at[r], to_x(r))
        cp.start()
        cx.append(cp)
    cov_prod = product(x)
    load_s.wait()
    for cp in cx:
        cp.wait_recv()
    for r in range(1, 4):
        cov_prod = cov_prod + cx_r[r].astype(F32)

    values = xj[x].astype(F32)
    centered = values - mean_j
    factor = N * D / loss_share
    invariance = 2.0 * inv_weight / (N * D) * (values - svb[...].astype(F32))
    spread_term = -var_weight / D * hinge * centered / ((N - 1) * deviation)
    cov_term = 4.0 * cov_weight / (D * (N - 1)) * (cov_prod / (N - 1) - centered * variance)
    vg = (factor * (invariance + spread_term + cov_term)).astype(BF16)
    vg_out[...] = vg

    load_w.wait()
    load_p.wait()

    def back(r, core):
        at = pl.multiple_of((((yl + r) % 4) * 2 + core) * COLS, COLS)
        return lax.dot_general(
            vg_out[...], wb[pl.ds(at, COLS), :], NT, preferred_element_type=F32)

    db = {}
    for r in (2, 1, 3, 0):
        db_s[r] = back(r, 1 - c).astype(BF16)
        db[r] = remote(db_s.at[r], db_r.at[r], db_ss.at[r], db_rs.at[r], partner)
        db[r].start()
    bk = []
    for r in (2, 1, 3, 0):
        mine = back(r, c)
        db[r].wait_recv()
        mine = mine + db_r[r].astype(F32)
        if r == 0:
            keep[...] = mine
        else:
            bk_s[r] = mine.astype(BF16)
            cp = remote(bk_s.at[r], bk_r.at[r], bk_ss.at[r], bk_rs.at[r], to_yl(r))
            cp.start()
            bk.append(cp)
    for cp in bk:
        cp.wait_recv()
    total = keep[...]
    for r in range(1, 4):
        total = total + bk_r[r].astype(F32)
    pg_out[...] = jnp.where(pab[...] > 0, total, 0.0).astype(BF16)

    for cp in s1j + s1k[1:] + gj + gk[1:] + s2 + s3 + [share] + swap + cx + bk:
        cp.wait_send()
    for group in (rs, ag, db):
        for cp in group.values():
            cp.wait_send()

    @pl.when(jnp.logical_not(diagonal))
    def _():
        s1k[0].wait_send()
        gk[0].wait_send()


def on_device(first_view, second_view, weight, pre_act):
    dma = pltpu.SemaphoreType.DMA
    vmem = pltpu.VMEM
    return pl.pallas_call(
        kernel,
        out_shape=[jax.ShapeDtypeStruct((ROWS, COLS), BF16)] * 2,
        in_specs=[pl.BlockSpec(memory_space=pl.ANY)] * 4,
        out_specs=[pl.BlockSpec(memory_space=pltpu.VMEM)] * 2,
        scratch_shapes=[
            vmem((4, ROWS, COLS), BF16),
            vmem((4, ROWS, COLS), BF16),
            vmem((4, ROWS, COLS), BF16),
            vmem((2, 4, ROWS, COLS), BF16),
            vmem((ROWS, COLS), BF16),
            vmem((D, COLS), BF16),
            vmem((ROWS, COLS), BF16),
            vmem((1, COLS), F32),
            vmem((2, 4, 1, COLS), F32),
            vmem((2, 1, COLS), F32),
            vmem((16, 2, 1, COLS), F32),
            vmem((1, COLS), F32),
            vmem((16, 1, COLS), F32),
            vmem((2, 8, UNIT, COLS), F32),
            vmem((2, 7, UNIT, COLS), BF16),
            vmem((2, 7, UNIT, COLS), BF16),
            vmem((2, UNIT, COLS), BF16),
            vmem((2, UNIT, COLS), BF16),
            vmem((2, 8, UNIT, COLS), BF16),
            vmem((4, ROWS, COLS), BF16),
            vmem((4, ROWS, COLS), BF16),
            vmem((4, ROWS, COLS), BF16),
            vmem((4, ROWS, COLS), BF16),
            vmem((4, ROWS, COLS), BF16),
            vmem((4, ROWS, COLS), BF16),
            vmem((ROWS, COLS), F32),
            dma((5,)),
            dma((4,)), dma((4,)), dma((4,)), dma((4,)),
            dma((2, 4)), dma((2, 4)), dma((16,)), dma((16,)), dma((16,)), dma((16,)),
            dma, dma, dma((2, 7)), dma((2, 7)), dma((2,)), dma((2,)), dma((2, 7)), dma((2, 7)),
            dma((4,)), dma((4,)), dma((4,)), dma((4,)), dma((4,)), dma((4,)),
        ],
        compiler_params=pltpu.CompilerParams(
            collective_id=0, has_side_effects=True, vmem_limit_bytes=48 * 2**20),
        cost_estimate=pl.CostEstimate(flops=2700000000, bytes_accessed=5000000, transcendentals=0),
        name="vicreg_backward",
    )(first_view, second_view, weight, pre_act)


def solution(mesh):
    return jax.shard_map(
        on_device,
        mesh=mesh,
        in_specs=(P("pairs", "dims"), P("pairs", "dims"), P(None, "dims"), P("pairs", "dims")),
        out_specs=(P("pairs", "dims"), P("pairs", "dims")),
        check_vma=False,
    )
```

```python
import jax
import jax.numpy as jnp
from jax import lax
from jax.experimental import pallas as pl
from jax.experimental.pallas import tpu as pltpu
from jax.sharding import PartitionSpec as P

D = 4096
N = 8192
ROWS = 128
COLS = 512
UNIT = 32

inv_weight = 25.0
var_weight = 25.0
cov_weight = 1.0
var_eps = 1e-05
loss_share = 32.0

F32 = jnp.float32
BF16 = jnp.bfloat16
NT = (((1,), (1,)), ((), ()))
TN = (((0,), (0,)), ((), ()))


def kernel(
    fv, sv, w, pa, vg_out, pg_out,
    xj, xk, pj, pk, svb, wb, pab,
    own, st1, tot, st2, msq, st3,
    cf, rs_s, rs_r, yh_s, yh_r, call,
    cov, cx_s, cx_r, db_s, db_r, bk_s, bk_r, keep,
    lsem,
    xj_ss, xj_rs, xk_ss, xk_rs,
    s1_ss, s1_rs, s2_ss, s2_rs, s3_ss, s3_rs,
    pk_ss, pk_rs, rsz_ss, rsz_rs, yh_ss, yh_rs, ag_ss, ag_rs,
    cx_ss, cx_rs, db_ss, db_rs, bk_ss, bk_rs,
):
    p = lax.axis_index("pairs")
    d = lax.axis_index("dims")
    z, yh, x = p // 8, (p // 4) % 2, p % 4
    yl, c = d // 2, d % 2

    def dev(z_, yh_, x_, yl_, c_):
        return (z_ * 8 + yh_ * 4 + x_, yl_ * 2 + c_)

    def to_x(r):
        return dev(z, yh, (x + r) % 4, yl, c)

    def to_k(r):
        return dev(z, yh, yl, (x + r) % 4, c)

    def from_k(r):
        return dev(z, yh, (yl + 4 - r) % 4, x, c)

    def to_yl(r):
        return dev(z, yh, x, (yl + r) % 4, c)

    def to_zy(r):
        return dev((z + r % 8) % 8, (yh + r // 8) % 2, x, yl, c)

    partner = dev(z, yh, x, yl, 1 - c)
    diagonal = x == yl

    def remote(src, dst, ss, rs, to):
        return pltpu.make_async_remote_copy(
            src_ref=src, dst_ref=dst, send_sem=ss, recv_sem=rs,
            device_id=to, device_id_type=pl.DeviceIdType.MESH)

    load_x = pltpu.make_async_copy(fv, xj.at[x], lsem.at[0])
    load_x.start()
    load_w = pltpu.make_async_copy(w, wb, lsem.at[1])
    load_s = pltpu.make_async_copy(sv, svb, lsem.at[2])
    load_p = pltpu.make_async_copy(pa, pab, lsem.at[3])
    load_k = pltpu.make_async_copy(fv, xk.at[x], lsem.at[4])

    barrier = pltpu.get_barrier_semaphore()

    def greet(to):
        pl.semaphore_signal(barrier, inc=1, device_id=to, device_id_type=pl.DeviceIdType.MESH)

    count = 0
    for r in range(1, 16):
        greet(to_zy(r))
        count += 1
    for r in range(1, 4):
        greet(to_x(r))
        greet(to_k(r))
        greet(from_k(r))
        greet(to_yl(r))
        count += 4
    greet(partner)
    count += 1

    @pl.when(jnp.logical_not(diagonal))
    def _():
        greet(to_k(0))
        greet(from_k(0))

    @pl.when(diagonal)
    def _():
        load_k.start()

    load_w.start()
    load_s.start()
    load_p.start()
    load_x.wait()
    own[...] = jnp.sum(xj[x].astype(F32), axis=0, keepdims=True)

    @pl.when(jnp.logical_not(diagonal))
    def _():
        pl.semaphore_wait(barrier, count + 2)

    @pl.when(diagonal)
    def _():
        pl.semaphore_wait(barrier, count)

    s1j = [remote(own, st1.at[0, r], s1_ss.at[0, r], s1_rs.at[0, r], to_x(r)) for r in range(1, 4)]
    s1k = [remote(own, st1.at[1, r], s1_ss.at[1, r], s1_rs.at[1, r], to_k(r)) for r in range(4)]
    gj = [remote(xj.at[x], xj.at[x], xj_ss.at[r], xj_rs.at[r], to_x(r)) for r in range(1, 4)]
    gk = [remote(xj.at[x], xk.at[x], xk_ss.at[r], xk_rs.at[r], to_k(r)) for r in range(4)]
    for cp in s1j + s1k[1:]:
        cp.start()

    @pl.when(jnp.logical_not(diagonal))
    def _():
        s1k[0].start()
        gk[0].start()

    for cp in gk[1:] + gj:
        cp.start()

    @pl.when(diagonal)
    def _():
        st1[1, 0] = own[...]

    for cp in s1j:
        cp.wait_recv()
    tot[0] = own[...] + st1[0, 1] + st1[0, 2] + st1[0, 3]

    @pl.when(jnp.logical_not(diagonal))
    def _():
        s1k[0].wait_recv()

    for cp in s1k[1:]:
        cp.wait_recv()
    tot[1] = st1[1, 0] + st1[1, 1] + st1[1, 2] + st1[1, 3]
    s2 = [remote(tot, st2.at[r], s2_ss.at[r], s2_rs.at[r], to_zy(r)) for r in range(1, 16)]
    for cp in s2:
        cp.start()
    for cp in s2:
        cp.wait_recv()
    mean = tot[...]
    for r in range(1, 16):
        mean = mean + st2[r]
    mean = mean / N
    mean_j, mean_k = mean[0], mean[1]

    for cp in gk[1:]:
        cp.wait_recv()

    @pl.when(jnp.logical_not(diagonal))
    def _():
        gk[0].wait_recv()

    @pl.when(diagonal)
    def _():
        load_k.wait()

    @pl.loop(0, 4)
    def _(b):
        pk[0, b] = (xk[b].astype(F32) - mean_k).astype(BF16)

    share = remote(pk.at[0], pk.at[1], pk_ss, pk_rs, partner)
    share.start()
    for cp in gj:
        cp.wait_recv()
    msq[...] = jnp.zeros_like(msq)

    @pl.loop(0, 4)
    def _(b):
        centered = xj[b].astype(F32) - mean_j
        pj[b] = centered.astype(BF16)
        msq[...] += jnp.sum(centered * centered, axis=0, keepdims=True)

    s3 = [remote(msq, st3.at[r], s3_ss.at[r], s3_rs.at[r], to_zy(r)) for r in range(1, 16)]

    def block(h):
        prod = lax.dot_general(
            pj[...].reshape(4 * ROWS, COLS), pk[h].reshape(4 * ROWS, COLS), TN,
            preferred_element_type=F32)
        cf[h] = prod.reshape(2, 8, UNIT, COLS)

    def along(way, hops):
        return dev((z + (hops if way == 0 else 8 - hops)) % 8, yh, x, yl, c)

    def unit(way, hops):
        return (z + (hops if way == 0 else 8 - hops)) % 8

    sent = []
    rs = {}

    def reduce_step(q, h, way, k):
        if k == 4 and h != way:
            return
        val = cf[h, q, unit(way, k)]
        for m in {2: (4, 3), 1: (2,)}.get(k, ()):
            if (q, h, way, m) in rs:
                rs[q, h, way, m].wait_recv()
                val = val + rs_r[q, h, way, m - 1].astype(F32)
        at = (q, h, way, k - 1)
        rs_s[at] = val.astype(BF16)
        cp = remote(rs_s.at[at], rs_r.at[at], rsz_ss.at[at], rsz_rs.at[at],
                    along(way, 2 if k == 4 else 1))
        cp.start()
        rs[q, h, way, k] = cp
        sent.append(cp)

    block(0)
    for q in range(2):
        for way in range(2):
            reduce_step(q, 0, way, 4)
            reduce_step(q, 0, way, 3)
    share.wait_recv()
    block(1)
    for q in range(2):
        for way in range(2):
            reduce_step(q, 1, way, 4)
            reduce_step(q, 1, way, 3)
    for cp in s3:
        cp.start()
    for k in (2, 1):
        for q in range(2):
            for h in range(2):
                for way in range(2):
                    reduce_step(q, h, way, k)

    swap = {}
    for q in range(2):
        for h in range(2):
            mine = cf[h, q, z]
            for way in range(2):
                rs[q, h, way, 1].wait_recv()
                mine = mine + rs_r[q, h, way, 0].astype(F32)
            cf[h, q, z] = mine
            yh_s[q, h] = mine.astype(BF16)
            cp = remote(yh_s.at[q, h], yh_r.at[q, h], yh_ss.at[q, h], yh_rs.at[q, h], to_zy(8))
            cp.start()
            swap[q, h] = cp
            sent.append(cp)

    ag = {}

    def gather_step(q, h, way, k):
        if k == 4 and h != way:
            return
        if k > 1 and k != 4:
            ag[q, h, way, k - 1].wait_recv()
        at = (q, h, way, k - 1)
        held = call.at[h, q, unit(1 - way, min(k, 3) - 1)]
        cp = remote(held, held, ag_ss.at[at], ag_rs.at[at], along(way, 2 if k == 4 else 1))
        cp.start()
        ag[q, h, way, k] = cp
        sent.append(cp)

    for q in range(2):
        for h in range(2):
            swap[q, h].wait_recv()
            call[h, q, z] = (cf[h, q, z] + yh_r[q, h].astype(F32)).astype(BF16)
            for way in range(2):
                gather_step(q, h, way, 1)

    for cp in s3:
        cp.wait_recv()
    variance = msq[...]
    for r in range(1, 16):
        variance = variance + st3[r]
    variance = variance / (N - 1)
    deviation = jnp.sqrt(variance + var_eps)
    hinge = jnp.where(deviation < 1.0, 1.0, 0.0).astype(F32)
    for k in (2, 3):
        for q in range(2):
            for h in range(2):
                for way in range(2):
                    gather_step(q, h, way, k)
                    if k == 3:
                        gather_step(q, h, way, 4)

    cx = {}

    def product(q):
        for h in range(2):
            for way in range(2):
                ag[q, h, way, 3].wait_recv()
                if h == way:
                    ag[q, h, way, 4].wait_recv()
        out = lax.dot_general(
            pk[0].reshape(4 * ROWS, COLS), call[0, q].reshape(COLS // 2, COLS), NT,
            preferred_element_type=F32)
        out = out + lax.dot_general(
            pk[1].reshape(4 * ROWS, COLS), call[1, q].reshape(COLS // 2, COLS), NT,
            preferred_element_type=F32)
        cov[q] = out.reshape(4, ROWS, COLS // 2)
        for r in (2, 1, 3):
            cx_s[q, r] = cov[q, (x + r) % 4].astype(BF16)
            cp = remote(cx_s.at[q, r], cx_r.at[q, r], cx_ss.at[q, r], cx_rs.at[q, r], to_x(r))
            cp.start()
            cx[q, r] = cp
            sent.append(cp)

    product(0)
    product(1)
    load_s.wait()
    factor = N * D / loss_share
    for q in range(2):
        at = slice(q * COLS // 2, (q + 1) * COLS // 2)
        cov_prod = cov[q, x]
        for r in range(1, 4):
            cx[q, r].wait_recv()
            cov_prod = cov_prod + cx_r[q, r].astype(F32)
        values = xj[x, :, at].astype(F32)
        centered = values - mean_j[:, at]
        invariance = 2.0 * inv_weight / (N * D) * (values - svb[:, at].astype(F32))
        spread_term = -var_weight / D * hinge[:, at] * centered / ((N - 1) * deviation[:, at])
        cov_term = 4.0 * cov_weight / (D * (N - 1)) * (cov_prod / (N - 1) - centered * variance[:, at])
        vg_out[:, at] = (factor * (invariance + spread_term + cov_term)).astype(BF16)

    load_w.wait()
    load_p.wait()

    def back(r, core):
        at = pl.multiple_of((((yl + r) % 4) * 2 + core) * COLS, COLS)
        return lax.dot_general(
            vg_out[...], wb[pl.ds(at, COLS), :], NT, preferred_element_type=F32)

    db = {}
    bk = []

    def lend(r):
        db_s[r] = back(r, 1 - c).astype(BF16)
        db[r] = remote(db_s.at[r], db_r.at[r], db_ss.at[r], db_rs.at[r], partner)
        db[r].start()
        sent.append(db[r])

    def send_back(r):
        mine = back(r, c)
        db[r].wait_recv()
        mine = mine + db_r[r].astype(F32)
        if r == 0:
            keep[...] = mine
        else:
            bk_s[r] = mine.astype(BF16)
            cp = remote(bk_s.at[r], bk_r.at[r], bk_ss.at[r], bk_rs.at[r], to_yl(r))
            cp.start()
            bk.append(cp)
            sent.append(cp)

    lend(2)
    lend(1)
    send_back(2)
    lend(3)
    send_back(1)
    lend(0)
    send_back(3)
    send_back(0)
    for cp in bk:
        cp.wait_recv()
    total = keep[...]
    for r in range(1, 4):
        total = total + bk_r[r].astype(F32)
    pg_out[...] = jnp.where(pab[...] > 0, total, 0.0).astype(BF16)

    for cp in s1j + s1k[1:] + gj + gk[1:] + s2 + s3 + [share] + sent:
        cp.wait_send()

    @pl.when(jnp.logical_not(diagonal))
    def _():
        s1k[0].wait_send()
        gk[0].wait_send()


def on_device(first_view, second_view, weight, pre_act):
    dma = pltpu.SemaphoreType.DMA
    vmem = pltpu.VMEM
    return pl.pallas_call(
        kernel,
        out_shape=[jax.ShapeDtypeStruct((ROWS, COLS), BF16)] * 2,
        in_specs=[pl.BlockSpec(memory_space=pltpu.HBM)] * 4,
        out_specs=[pl.BlockSpec(memory_space=pltpu.VMEM)] * 2,
        scratch_shapes=[
            vmem((4, ROWS, COLS), BF16),
            vmem((4, ROWS, COLS), BF16),
            vmem((4, ROWS, COLS), BF16),
            vmem((2, 4, ROWS, COLS), BF16),
            vmem((ROWS, COLS), BF16),
            vmem((D, COLS), BF16),
            vmem((ROWS, COLS), BF16),
            vmem((1, COLS), F32),
            vmem((2, 4, 1, COLS), F32),
            vmem((2, 1, COLS), F32),
            vmem((16, 2, 1, COLS), F32),
            vmem((1, COLS), F32),
            vmem((16, 1, COLS), F32),
            vmem((2, 2, 8, UNIT, COLS), F32),
            vmem((2, 2, 2, 4, UNIT, COLS), BF16),
            vmem((2, 2, 2, 4, UNIT, COLS), BF16),
            vmem((2, 2, UNIT, COLS), BF16),
            vmem((2, 2, UNIT, COLS), BF16),
            vmem((2, 2, 8, UNIT, COLS), BF16),
            vmem((2, 4, ROWS, COLS // 2), F32),
            vmem((2, 4, ROWS, COLS // 2), BF16),
            vmem((2, 4, ROWS, COLS // 2), BF16),
            vmem((4, ROWS, COLS), BF16),
            vmem((4, ROWS, COLS), BF16),
            vmem((4, ROWS, COLS), BF16),
            vmem((4, ROWS, COLS), BF16),
            vmem((ROWS, COLS), F32),
            dma((5,)),
            dma((4,)), dma((4,)), dma((4,)), dma((4,)),
            dma((2, 4)), dma((2, 4)), dma((16,)), dma((16,)), dma((16,)), dma((16,)),
            dma, dma, dma((2, 2, 2, 4)), dma((2, 2, 2, 4)), dma((2, 2)), dma((2, 2)),
            dma((2, 2, 2, 4)), dma((2, 2, 2, 4)),
            dma((2, 4)), dma((2, 4)), dma((4,)), dma((4,)), dma((4,)), dma((4,)),
        ],
        compiler_params=pltpu.CompilerParams(
            collective_id=0, has_side_effects=True, vmem_limit_bytes=60 * 2**20),
        cost_estimate=pl.CostEstimate(flops=2700000000, bytes_accessed=5000000, transcendentals=0),
        name="vicreg_backward",
    )(first_view, second_view, weight, pre_act)


def solution(mesh):
    return jax.shard_map(
        on_device,
        mesh=mesh,
        in_specs=(P("pairs", "dims"), P("pairs", "dims"), P(None, "dims"), P("pairs", "dims")),
        out_specs=(P("pairs", "dims"), P("pairs", "dims")),
        check_vma=False,
    )
```

```python
import jax
import jax.numpy as jnp
from jax import lax
from jax.experimental import pallas as pl
from jax.experimental.pallas import tpu as pltpu
from jax.sharding import PartitionSpec as P

D = 4096
N = 8192
ROWS = 128
HALF = 64
COLS = 512
UNIT = 32

inv_weight = 25.0
var_weight = 25.0
cov_weight = 1.0
var_eps = 1e-05
loss_share = 32.0

F32 = jnp.float32
BF16 = jnp.bfloat16
NT = (((1,), (1,)), ((), ()))
TN = (((0,), (0,)), ((), ()))


def kernel(
    fv, sv, w, pa, vg_out, pg_out,
    xj, xk, pj, pk, svb, wb, pab,
    own, st1, tot, st2, msq, st3,
    cf, rs_s, rs_r, yh_s, yh_r, call,
    cov, cx_s, cx_r, vgp, bk_s, bk_r, keep,
    lsem,
    xj_ss, xj_rs, xk_ss, xk_rs,
    s1_ss, s1_rs, s2_ss, s2_rs, s3_ss, s3_rs,
    pk_ss, pk_rs, rsz_ss, rsz_rs, yh_ss, yh_rs, ag_ss, ag_rs,
    cx_ss, cx_rs, vg_ss, vg_rs, bk_ss, bk_rs, w_sem, w_ss, w_rs,
):
    p = lax.axis_index("pairs")
    d = lax.axis_index("dims")
    z, yh, x = p // 8, (p // 4) % 2, p % 4
    yl, c = d // 2, d % 2

    def dev(z_, yh_, x_, yl_, c_):
        return (z_ * 8 + yh_ * 4 + x_, yl_ * 2 + c_)

    def to_x(r):
        return dev(z, yh, (x + r) % 4, yl, c)

    def to_k(r):
        return dev(z, yh, yl, (x + r) % 4, c)

    def from_k(r):
        return dev(z, yh, (yl + 4 - r) % 4, x, c)

    def to_yl(r):
        return dev(z, yh, x, (yl + r) % 4, c)

    def to_zy(r):
        return dev((z + r % 8) % 8, (yh + r // 8) % 2, x, yl, c)

    partner = dev(z, yh, x, yl, 1 - c)
    diagonal = x == yl

    def remote(src, dst, ss, rs, to):
        return pltpu.make_async_remote_copy(
            src_ref=src, dst_ref=dst, send_sem=ss, recv_sem=rs,
            device_id=to, device_id_type=pl.DeviceIdType.MESH)

    load_x = pltpu.make_async_copy(fv, xj.at[x], lsem.at[0])
    load_x.start()
    load_w = [
        pltpu.make_async_copy(w.at[i * 2 + c], wb.at[i, 0], w_sem.at[i]) for i in range(4)]
    load_s = pltpu.make_async_copy(sv, svb, lsem.at[2])
    load_p = pltpu.make_async_copy(pa, pab, lsem.at[3])
    load_k = pltpu.make_async_copy(fv, xk.at[x], lsem.at[4])

    barrier = pltpu.get_barrier_semaphore()

    def greet(to):
        pl.semaphore_signal(barrier, inc=1, device_id=to, device_id_type=pl.DeviceIdType.MESH)

    count = 0
    for r in range(1, 16):
        greet(to_zy(r))
        count += 1
    for r in range(1, 4):
        greet(to_x(r))
        greet(to_k(r))
        greet(from_k(r))
        greet(to_yl(r))
        count += 4
    greet(partner)
    count += 1

    @pl.when(jnp.logical_not(diagonal))
    def _():
        greet(to_k(0))
        greet(from_k(0))

    @pl.when(diagonal)
    def _():
        load_k.start()

    for cp in load_w:
        cp.start()
    load_s.start()
    load_p.start()
    load_x.wait()
    own[...] = jnp.sum(xj[x].astype(F32), axis=0, keepdims=True)

    @pl.when(jnp.logical_not(diagonal))
    def _():
        pl.semaphore_wait(barrier, count + 2)

    @pl.when(diagonal)
    def _():
        pl.semaphore_wait(barrier, count)

    s1j = [remote(own, st1.at[0, r], s1_ss.at[0, r], s1_rs.at[0, r], to_x(r)) for r in range(1, 4)]
    s1k = [remote(own, st1.at[1, r], s1_ss.at[1, r], s1_rs.at[1, r], to_k(r)) for r in range(4)]
    gj = [remote(xj.at[x], xj.at[x], xj_ss.at[r], xj_rs.at[r], to_x(r)) for r in range(1, 4)]
    gk = [remote(xj.at[x], xk.at[x], xk_ss.at[r], xk_rs.at[r], to_k(r)) for r in range(4)]
    for cp in s1j + s1k[1:]:
        cp.start()

    @pl.when(jnp.logical_not(diagonal))
    def _():
        s1k[0].start()
        gk[0].start()

    for cp in gk[1:] + gj:
        cp.start()

    lend_w = [
        remote(w.at[i * 2 + 1 - c], wb.at[i, 1], w_ss.at[i], w_rs.at[i], partner) for i in range(4)]
    for cp in lend_w:
        cp.start()

    @pl.when(diagonal)
    def _():
        st1[1, 0] = own[...]

    for cp in s1j:
        cp.wait_recv()
    tot[0] = own[...] + st1[0, 1] + st1[0, 2] + st1[0, 3]

    @pl.when(jnp.logical_not(diagonal))
    def _():
        s1k[0].wait_recv()

    for cp in s1k[1:]:
        cp.wait_recv()
    tot[1] = st1[1, 0] + st1[1, 1] + st1[1, 2] + st1[1, 3]
    s2 = [remote(tot, st2.at[r], s2_ss.at[r], s2_rs.at[r], to_zy(r)) for r in range(1, 16)]
    for cp in s2:
        cp.start()
    for cp in s2:
        cp.wait_recv()
    mean = tot[...]
    for r in range(1, 16):
        mean = mean + st2[r]
    mean = mean / N
    mean_j, mean_k = mean[0], mean[1]

    for cp in gk[1:]:
        cp.wait_recv()

    @pl.when(jnp.logical_not(diagonal))
    def _():
        gk[0].wait_recv()

    @pl.when(diagonal)
    def _():
        load_k.wait()

    @pl.loop(0, 4)
    def _(b):
        pk[0, b] = (xk[b].astype(F32) - mean_k).astype(BF16)

    share = remote(pk.at[0], pk.at[1], pk_ss, pk_rs, partner)
    share.start()
    for cp in gj:
        cp.wait_recv()
    msq[...] = jnp.zeros_like(msq)

    @pl.loop(0, 4)
    def _(b):
        centered = xj[b].astype(F32) - mean_j
        pj[b] = centered.astype(BF16)
        msq[...] += jnp.sum(centered * centered, axis=0, keepdims=True)

    s3 = [remote(msq, st3.at[r], s3_ss.at[r], s3_rs.at[r], to_zy(r)) for r in range(1, 16)]

    def block(h):
        prod = lax.dot_general(
            pj[...].reshape(4 * ROWS, COLS), pk[h].reshape(4 * ROWS, COLS), TN,
            preferred_element_type=F32)
        cf[h] = prod.reshape(2, 8, UNIT, COLS)

    def along(way, hops):
        return dev((z + (hops if way == 0 else 8 - hops)) % 8, yh, x, yl, c)

    def unit(way, hops):
        return (z + (hops if way == 0 else 8 - hops)) % 8

    sent = []
    rs = {}

    def reduce_step(q, h, way, k):
        if k == 4 and h != way:
            return
        val = cf[h, q, unit(way, k)]
        for m in {2: (4, 3), 1: (2,)}.get(k, ()):
            if (q, h, way, m) in rs:
                rs[q, h, way, m].wait_recv()
                val = val + rs_r[q, h, way, m - 1].astype(F32)
        at = (q, h, way, k - 1)
        rs_s[at] = val.astype(BF16)
        cp = remote(rs_s.at[at], rs_r.at[at], rsz_ss.at[at], rsz_rs.at[at],
                    along(way, 2 if k == 4 else 1))
        cp.start()
        rs[q, h, way, k] = cp
        sent.append(cp)

    block(0)
    for q in range(2):
        for way in range(2):
            reduce_step(q, 0, way, 4)
            reduce_step(q, 0, way, 3)
    share.wait_recv()
    block(1)
    for q in range(2):
        for way in range(2):
            reduce_step(q, 1, way, 4)
            reduce_step(q, 1, way, 3)
    for cp in s3:
        cp.start()
    for k in (2, 1):
        for q in range(2):
            for h in range(2):
                for way in range(2):
                    reduce_step(q, h, way, k)

    swap = {}
    for q in range(2):
        for h in range(2):
            mine = cf[h, q, z]
            for way in range(2):
                rs[q, h, way, 1].wait_recv()
                mine = mine + rs_r[q, h, way, 0].astype(F32)
            cf[h, q, z] = mine
            yh_s[q, h] = mine.astype(BF16)
            cp = remote(yh_s.at[q, h], yh_r.at[q, h], yh_ss.at[q, h], yh_rs.at[q, h], to_zy(8))
            cp.start()
            swap[q, h] = cp
            sent.append(cp)

    ag = {}

    def gather_step(q, h, way, k):
        if k == 4 and h != way:
            return
        if k > 1 and k != 4:
            ag[q, h, way, k - 1].wait_recv()
        at = (q, h, way, k - 1)
        held = call.at[h, q, unit(1 - way, min(k, 3) - 1)]
        cp = remote(held, held, ag_ss.at[at], ag_rs.at[at], along(way, 2 if k == 4 else 1))
        cp.start()
        ag[q, h, way, k] = cp
        sent.append(cp)

    for q in range(2):
        for h in range(2):
            swap[q, h].wait_recv()
            call[h, q, z] = (cf[h, q, z] + yh_r[q, h].astype(F32)).astype(BF16)
            for way in range(2):
                gather_step(q, h, way, 1)

    for cp in s3:
        cp.wait_recv()
    variance = msq[...]
    for r in range(1, 16):
        variance = variance + st3[r]
    variance = variance / (N - 1)
    deviation = jnp.sqrt(variance + var_eps)
    hinge = jnp.where(deviation < 1.0, 1.0, 0.0).astype(F32)
    for k in (2, 3):
        for q in range(2):
            for h in range(2):
                for way in range(2):
                    gather_step(q, h, way, k)
                    if k == 3:
                        gather_step(q, h, way, 4)

    cx = {}
    halves = (slice(0, HALF), slice(HALF, ROWS))

    def product(q):
        for h in range(2):
            for way in range(2):
                ag[q, h, way, 3].wait_recv()
                if h == way:
                    ag[q, h, way, 4].wait_recv()
        out = lax.dot_general(
            pk[0].reshape(4 * ROWS, COLS), call[0, q].reshape(COLS // 2, COLS), NT,
            preferred_element_type=F32)
        out = out + lax.dot_general(
            pk[1].reshape(4 * ROWS, COLS), call[1, q].reshape(COLS // 2, COLS), NT,
            preferred_element_type=F32)
        cov[q] = out.reshape(4, ROWS, COLS // 2)
        for rows in ((slice(0, ROWS),) if q == 0 else halves):
            part = rows.start // HALF
            for r in (2, 1, 3):
                cx_s[q, r, rows] = cov[q, (x + r) % 4, rows].astype(BF16)
                cp = remote(cx_s.at[q, r, rows], cx_r.at[q, r, rows], cx_ss.at[q, r, part],
                            cx_rs.at[q, r, part], to_x(r))
                cp.start()
                cx[q, r, part] = cp
                sent.append(cp)

    product(0)
    product(1)
    load_s.wait()
    factor = N * D / loss_share
    vgc = {}

    def view_grad(q, part):
        at = slice(q * COLS // 2, (q + 1) * COLS // 2)
        rows = halves[part]
        cov_prod = cov[q, x, rows]
        for r in range(1, 4):
            if (q, r, part) in cx:
                cx[q, r, part].wait_recv()
            cov_prod = cov_prod + cx_r[q, r, rows].astype(F32)
        values = xj[x, rows, at].astype(F32)
        centered = values - mean_j[:, at]
        invariance = 2.0 * inv_weight / (N * D) * (values - svb[rows, at].astype(F32))
        spread_term = -var_weight / D * hinge[:, at] * centered / ((N - 1) * deviation[:, at])
        cov_term = 4.0 * cov_weight / (D * (N - 1)) * (cov_prod / (N - 1) - centered * variance[:, at])
        vg_out[rows, at] = (factor * (invariance + spread_term + cov_term)).astype(BF16)
        cp = remote(vg_out.at[rows, at], vgp.at[rows, at], vg_ss.at[q, part], vg_rs.at[q, part], partner)
        cp.start()
        vgc[q, part] = cp
        sent.append(cp)

    bk = []

    def back(part, r):
        rows = halves[part]
        at = (yl + r) % 4
        out = lax.dot_general(vg_out[rows], wb[at, 0], NT, preferred_element_type=F32)
        return out + lax.dot_general(vgp[rows], wb[at, 1], NT, preferred_element_type=F32)

    def send_back(part):
        rows = halves[part]
        for q in range(2):
            vgc[q, part].wait_recv()
        for r in (2, 1, 3):
            bk_s[r, rows] = back(part, r).astype(BF16)
            cp = remote(bk_s.at[r, rows], bk_r.at[r, rows], bk_ss.at[r, part], bk_rs.at[r, part], to_yl(r))
            cp.start()
            bk.append(cp)
            sent.append(cp)

    view_grad(0, 0)
    view_grad(0, 1)
    view_grad(1, 0)
    for cp in load_w:
        cp.wait()
    for cp in lend_w:
        cp.wait_recv()
    send_back(0)
    view_grad(1, 1)
    send_back(1)
    for part in range(2):
        keep[halves[part]] = back(part, 0)
    load_p.wait()
    for cp in bk:
        cp.wait_recv()
    total = keep[...]
    for r in range(1, 4):
        total = total + bk_r[r].astype(F32)
    pg_out[...] = jnp.where(pab[...] > 0, total, 0.0).astype(BF16)

    for cp in s1j + s1k[1:] + gj + gk[1:] + s2 + s3 + [share] + lend_w + sent:
        cp.wait_send()

    @pl.when(jnp.logical_not(diagonal))
    def _():
        s1k[0].wait_send()
        gk[0].wait_send()


def backward(first_view, second_view, weight, pre_act):
    dma = pltpu.SemaphoreType.DMA
    vmem = pltpu.VMEM
    return pl.pallas_call(
        kernel,
        out_shape=[jax.ShapeDtypeStruct((ROWS, COLS), BF16)] * 2,
        in_specs=[pl.BlockSpec(memory_space=pltpu.HBM)] * 4,
        out_specs=[pl.BlockSpec(memory_space=pltpu.VMEM)] * 2,
        scratch_shapes=[
            vmem((4, ROWS, COLS), BF16),
            vmem((4, ROWS, COLS), BF16),
            vmem((4, ROWS, COLS), BF16),
            vmem((2, 4, ROWS, COLS), BF16),
            vmem((ROWS, COLS), BF16),
            vmem((4, 2, COLS, COLS), BF16),
            vmem((ROWS, COLS), BF16),
            vmem((1, COLS), F32),
            vmem((2, 4, 1, COLS), F32),
            vmem((2, 1, COLS), F32),
            vmem((16, 2, 1, COLS), F32),
            vmem((1, COLS), F32),
            vmem((16, 1, COLS), F32),
            vmem((2, 2, 8, UNIT, COLS), F32),
            vmem((2, 2, 2, 4, UNIT, COLS), BF16),
            vmem((2, 2, 2, 4, UNIT, COLS), BF16),
            vmem((2, 2, UNIT, COLS), BF16),
            vmem((2, 2, UNIT, COLS), BF16),
            vmem((2, 2, 8, UNIT, COLS), BF16),
            vmem((2, 4, ROWS, COLS // 2), F32),
            vmem((2, 4, ROWS, COLS // 2), BF16),
            vmem((2, 4, ROWS, COLS // 2), BF16),
            vmem((ROWS, COLS), BF16),
            vmem((4, ROWS, COLS), BF16),
            vmem((4, ROWS, COLS), BF16),
            vmem((ROWS, COLS), F32),
            dma((5,)),
            dma((4,)), dma((4,)), dma((4,)), dma((4,)),
            dma((2, 4)), dma((2, 4)), dma((16,)), dma((16,)), dma((16,)), dma((16,)),
            dma, dma, dma((2, 2, 2, 4)), dma((2, 2, 2, 4)), dma((2, 2)), dma((2, 2)),
            dma((2, 2, 2, 4)), dma((2, 2, 2, 4)),
            dma((2, 4, 2)), dma((2, 4, 2)), dma((2, 2)), dma((2, 2)), dma((4, 2)), dma((4, 2)),
            dma((4,)), dma((4,)), dma((4,)),
        ],
        compiler_params=pltpu.CompilerParams(
            collective_id=0, has_side_effects=True, vmem_limit_bytes=60 * 2**20),
        cost_estimate=pl.CostEstimate(flops=2700000000, bytes_accessed=5000000, transcendentals=0),
        name="vicreg_backward",
    )(first_view, second_view, weight.reshape(8, COLS, COLS), pre_act)


def store_kernel(a, b, a_out, b_out, sems):
    copies = []
    for i in range(4):
        rows = slice(i * 32, (i + 1) * 32)
        copies.append(pltpu.make_async_copy(a.at[rows], a_out.at[rows], sems.at[0, i]))
        copies.append(pltpu.make_async_copy(b.at[rows], b_out.at[rows], sems.at[1, i]))
    for cp in copies:
        cp.start()
    for cp in copies:
        cp.wait()


def on_device(*args):
    return pl.pallas_call(
        store_kernel,
        out_shape=[jax.ShapeDtypeStruct((ROWS, COLS), BF16)] * 2,
        in_specs=[pl.BlockSpec(memory_space=pl.ANY)] * 2,
        out_specs=[pl.BlockSpec(memory_space=pl.ANY)] * 2,
        scratch_shapes=[pltpu.SemaphoreType.DMA((2, 4))],
        compiler_params=pltpu.CompilerParams(vmem_limit_bytes=60 * 2**20),
        name="store",
    )(*backward(*args))


def solution(mesh):
    return jax.shard_map(
        on_device,
        mesh=mesh,
        in_specs=(P("pairs", "dims"), P("pairs", "dims"), P(None, "dims"), P("pairs", "dims")),
        out_specs=(P("pairs", "dims"), P("pairs", "dims")),
        check_vma=False,
    )
```

```python
import jax
import jax.numpy as jnp
from jax import lax
from jax.experimental import pallas as pl
from jax.experimental.pallas import tpu as pltpu
from jax.sharding import PartitionSpec as P

D = 4096
N = 8192
ROWS = 128
COLS = 512
UNIT = 32

inv_weight = 25.0
var_weight = 25.0
cov_weight = 1.0
var_eps = 1e-05
loss_share = 32.0

F32 = jnp.float32
BF16 = jnp.bfloat16
NT = (((1,), (1,)), ((), ()))
TN = (((0,), (0,)), ((), ()))


def kernel(
    fv, sv, w, pa, vg_out, pg_out,
    xj, xk, pj, pk, svb, wb, pab,
    own, st1, tot, st2, msq, st3,
    cf, rs_s, rs_r, yh_s, yh_r, call,
    cov, cx_s, cx_r, vgp, bk_s, bk_r, keep,
    lsem,
    xj_ss, xj_rs, xk_ss, xk_rs,
    s1_ss, s1_rs, s2_ss, s2_rs, s3_ss, s3_rs,
    pk_ss, pk_rs, rsz_ss, rsz_rs, yh_ss, yh_rs, ag_ss, ag_rs,
    cx_ss, cx_rs, vg_ss, vg_rs, bk_ss, bk_rs, w_sem, w_ss, w_rs,
):
    p = lax.axis_index("pairs")
    d = lax.axis_index("dims")
    z, yh, x = p // 8, (p // 4) % 2, p % 4
    yl, c = d // 2, d % 2

    def dev(z_, yh_, x_, yl_, c_):
        return (z_ * 8 + yh_ * 4 + x_, yl_ * 2 + c_)

    def to_x(r):
        return dev(z, yh, (x + r) % 4, yl, c)

    def to_k(r):
        return dev(z, yh, yl, (x + r) % 4, c)

    def from_k(r):
        return dev(z, yh, (yl + 4 - r) % 4, x, c)

    def to_yl(r):
        return dev(z, yh, x, (yl + r) % 4, c)

    def to_zy(r):
        return dev((z + r % 8) % 8, (yh + r // 8) % 2, x, yl, c)

    partner = dev(z, yh, x, yl, 1 - c)
    diagonal = x == yl

    def remote(src, dst, ss, rs, to):
        return pltpu.make_async_remote_copy(
            src_ref=src, dst_ref=dst, send_sem=ss, recv_sem=rs,
            device_id=to, device_id_type=pl.DeviceIdType.MESH)

    load_x = pltpu.make_async_copy(fv, xj.at[x], lsem.at[0])
    load_x.start()
    load_w = [
        pltpu.make_async_copy(w.at[i * 2 + c], wb.at[i, 0], w_sem.at[i]) for i in range(4)]
    load_s = pltpu.make_async_copy(sv, svb, lsem.at[2])
    load_p = pltpu.make_async_copy(pa, pab, lsem.at[3])
    load_k = pltpu.make_async_copy(fv, xk.at[x], lsem.at[4])

    barrier = pltpu.get_barrier_semaphore()

    def greet(to):
        pl.semaphore_signal(barrier, inc=1, device_id=to, device_id_type=pl.DeviceIdType.MESH)

    count = 0
    for r in range(1, 16):
        greet(to_zy(r))
        count += 1
    for r in range(1, 4):
        greet(to_x(r))
        greet(to_k(r))
        greet(from_k(r))
        greet(to_yl(r))
        count += 4
    greet(partner)
    count += 1

    @pl.when(jnp.logical_not(diagonal))
    def _():
        greet(to_k(0))
        greet(from_k(0))

    @pl.when(diagonal)
    def _():
        load_k.start()

    for cp in load_w:
        cp.start()
    load_s.start()
    load_p.start()
    load_x.wait()
    own[...] = jnp.sum(xj[x].astype(F32), axis=0, keepdims=True)

    @pl.when(jnp.logical_not(diagonal))
    def _():
        pl.semaphore_wait(barrier, count + 2)

    @pl.when(diagonal)
    def _():
        pl.semaphore_wait(barrier, count)

    s1j = [remote(own, st1.at[0, r], s1_ss.at[0, r], s1_rs.at[0, r], to_x(r)) for r in range(1, 4)]
    s1k = [remote(own, st1.at[1, r], s1_ss.at[1, r], s1_rs.at[1, r], to_k(r)) for r in range(4)]
    gj = [remote(xj.at[x], xj.at[x], xj_ss.at[r], xj_rs.at[r], to_x(r)) for r in range(1, 4)]
    gk = [remote(xj.at[x], xk.at[x], xk_ss.at[r], xk_rs.at[r], to_k(r)) for r in range(4)]
    for cp in s1j + s1k[1:]:
        cp.start()

    @pl.when(jnp.logical_not(diagonal))
    def _():
        s1k[0].start()
        gk[0].start()

    for cp in gk[1:] + gj:
        cp.start()

    lend_w = [
        remote(w.at[i * 2 + 1 - c], wb.at[i, 1], w_ss.at[i], w_rs.at[i], partner) for i in range(4)]
    for cp in lend_w:
        cp.start()

    @pl.when(diagonal)
    def _():
        st1[1, 0] = own[...]

    for cp in s1j:
        cp.wait_recv()
    tot[0] = own[...] + st1[0, 1] + st1[0, 2] + st1[0, 3]

    @pl.when(jnp.logical_not(diagonal))
    def _():
        s1k[0].wait_recv()

    for cp in s1k[1:]:
        cp.wait_recv()
    tot[1] = st1[1, 0] + st1[1, 1] + st1[1, 2] + st1[1, 3]
    s2 = [remote(tot, st2.at[r], s2_ss.at[r], s2_rs.at[r], to_zy(r)) for r in range(1, 16)]
    for cp in s2:
        cp.start()
    for cp in s2:
        cp.wait_recv()
    mean = tot[...]
    for r in range(1, 16):
        mean = mean + st2[r]
    mean = mean / N
    mean_j, mean_k = mean[0], mean[1]

    for cp in gk[1:]:
        cp.wait_recv()

    @pl.when(jnp.logical_not(diagonal))
    def _():
        gk[0].wait_recv()

    @pl.when(diagonal)
    def _():
        load_k.wait()

    @pl.loop(0, 4)
    def _(b):
        pk[0, b] = (xk[b].astype(F32) - mean_k).astype(BF16)

    share = remote(pk.at[0], pk.at[1], pk_ss, pk_rs, partner)
    share.start()
    for cp in gj:
        cp.wait_recv()
    msq[...] = jnp.zeros_like(msq)

    @pl.loop(0, 4)
    def _(b):
        centered = xj[b].astype(F32) - mean_j
        pj[b] = centered.astype(BF16)
        msq[...] += jnp.sum(centered * centered, axis=0, keepdims=True)

    s3 = [remote(msq, st3.at[r], s3_ss.at[r], s3_rs.at[r], to_zy(r)) for r in range(1, 16)]

    def block(h):
        prod = lax.dot_general(
            pj[...].reshape(4 * ROWS, COLS), pk[h].reshape(4 * ROWS, COLS), TN,
            preferred_element_type=F32)
        cf[h] = prod.reshape(2, 8, UNIT, COLS)

    def along(way, hops):
        return dev((z + (hops if way == 0 else 8 - hops)) % 8, yh, x, yl, c)

    def unit(way, hops):
        return (z + (hops if way == 0 else 8 - hops)) % 8

    sent = []
    rs = {}

    def reduce_step(q, h, way, k):
        if k == 4 and h != way:
            return
        val = cf[h, q, unit(way, k)]
        for m in {2: (4, 3), 1: (2,)}.get(k, ()):
            if (q, h, way, m) in rs:
                rs[q, h, way, m].wait_recv()
                val = val + rs_r[q, h, way, m - 1].astype(F32)
        at = (q, h, way, k - 1)
        rs_s[at] = val.astype(BF16)
        cp = remote(rs_s.at[at], rs_r.at[at], rsz_ss.at[at], rsz_rs.at[at],
                    along(way, 2 if k == 4 else 1))
        cp.start()
        rs[q, h, way, k] = cp
        sent.append(cp)

    def start_reduce(q, h):
        for way in range(2):
            reduce_step(q, h, way, 4)
            reduce_step(q, h, way, 3)

    block(0)
    start_reduce(0, 0)
    share.wait_recv()
    block(1)
    start_reduce(0, 1)
    start_reduce(1, 0)
    start_reduce(1, 1)
    for k in (2, 1):
        for q in range(2):
            for h in range(2):
                for way in range(2):
                    reduce_step(q, h, way, k)
    for cp in s3:
        cp.start()

    swap = {}
    for q in range(2):
        for h in range(2):
            mine = cf[h, q, z]
            for way in range(2):
                rs[q, h, way, 1].wait_recv()
                mine = mine + rs_r[q, h, way, 0].astype(F32)
            cf[h, q, z] = mine
            yh_s[q, h] = mine.astype(BF16)
            cp = remote(yh_s.at[q, h], yh_r.at[q, h], yh_ss.at[q, h], yh_rs.at[q, h], to_zy(8))
            cp.start()
            swap[q, h] = cp
            sent.append(cp)

    ag = {}

    def gather_step(q, h, way, k):
        if k == 4 and h != way:
            return
        if k > 1 and k != 4:
            ag[q, h, way, k - 1].wait_recv()
        at = (q, h, way, k - 1)
        held = call.at[h, q, unit(1 - way, min(k, 3) - 1)]
        cp = remote(held, held, ag_ss.at[at], ag_rs.at[at], along(way, 2 if k == 4 else 1))
        cp.start()
        ag[q, h, way, k] = cp
        sent.append(cp)

    for q in range(2):
        for h in range(2):
            swap[q, h].wait_recv()
            call[h, q, z] = (cf[h, q, z] + yh_r[q, h].astype(F32)).astype(BF16)
            for way in range(2):
                gather_step(q, h, way, 1)

    for k in (2, 3):
        for q in range(2):
            for h in range(2):
                for way in range(2):
                    gather_step(q, h, way, k)
                    if k == 3:
                        gather_step(q, h, way, 4)

    for cp in s3:
        cp.wait_recv()
    variance = msq[...]
    for r in range(1, 16):
        variance = variance + st3[r]
    variance = variance / (N - 1)
    deviation = jnp.sqrt(variance + var_eps)
    hinge = jnp.where(deviation < 1.0, 1.0, 0.0).astype(F32)
    cx = {}

    def product(q):
        for h in range(2):
            for way in range(2):
                ag[q, h, way, 3].wait_recv()
                if h == way:
                    ag[q, h, way, 4].wait_recv()
        out = lax.dot_general(
            pk[0].reshape(4 * ROWS, COLS), call[0, q].reshape(COLS // 2, COLS), NT,
            preferred_element_type=F32)
        out = out + lax.dot_general(
            pk[1].reshape(4 * ROWS, COLS), call[1, q].reshape(COLS // 2, COLS), NT,
            preferred_element_type=F32)
        cov[q] = out.reshape(4, ROWS, COLS // 2)
        for r in (2, 1, 3):
            cx_s[q, r] = cov[q, (x + r) % 4].astype(BF16)
            cp = remote(cx_s.at[q, r], cx_r.at[q, r], cx_ss.at[q, r], cx_rs.at[q, r], to_x(r))
            cp.start()
            cx[q, r] = cp
            sent.append(cp)

    product(0)
    product(1)
    load_s.wait()
    factor = N * D / loss_share
    vgc = []

    def view_grad(q):
        at = slice(q * COLS // 2, (q + 1) * COLS // 2)
        cov_prod = cov[q, x]
        for r in range(1, 4):
            cx[q, r].wait_recv()
            cov_prod = cov_prod + cx_r[q, r].astype(F32)
        values = xj[x, :, at].astype(F32)
        centered = values - mean_j[:, at]
        invariance = 2.0 * inv_weight / (N * D) * (values - svb[:, at].astype(F32))
        spread_term = -var_weight / D * hinge[:, at] * centered / ((N - 1) * deviation[:, at])
        cov_term = 4.0 * cov_weight / (D * (N - 1)) * (cov_prod / (N - 1) - centered * variance[:, at])
        vg_out[:, at] = (factor * (invariance + spread_term + cov_term)).astype(BF16)
        cp = remote(vg_out.at[:, at], vgp.at[:, at], vg_ss.at[q], vg_rs.at[q], partner)
        cp.start()
        vgc.append(cp)
        sent.append(cp)

    view_grad(0)
    view_grad(1)

    bk = []

    def back(r):
        at = (yl + r) % 4
        out = lax.dot_general(vg_out[...], wb[at, 0], NT, preferred_element_type=F32)
        if r == 2:
            for cp in vgc:
                cp.wait_recv()
        return out + lax.dot_general(vgp[...], wb[at, 1], NT, preferred_element_type=F32)

    for cp in load_w:
        cp.wait()
    for cp in lend_w:
        cp.wait_recv()
    for r in (2, 1, 3):
        bk_s[r] = back(r).astype(BF16)
        cp = remote(bk_s.at[r], bk_r.at[r], bk_ss.at[r], bk_rs.at[r], to_yl(r))
        cp.start()
        bk.append(cp)
        sent.append(cp)
    keep[...] = back(0)
    load_p.wait()
    for cp in bk:
        cp.wait_recv()
    total = keep[...]
    for r in range(1, 4):
        total = total + bk_r[r].astype(F32)
    pg_out[...] = jnp.where(pab[...] > 0, total, 0.0).astype(BF16)

    for cp in s1j + s1k[1:] + gj + gk[1:] + s2 + s3 + [share] + lend_w + sent:
        cp.wait_send()

    @pl.when(jnp.logical_not(diagonal))
    def _():
        s1k[0].wait_send()
        gk[0].wait_send()


def backward(first_view, second_view, weight, pre_act):
    dma = pltpu.SemaphoreType.DMA
    vmem = pltpu.VMEM
    return pl.pallas_call(
        kernel,
        out_shape=[jax.ShapeDtypeStruct((ROWS, COLS), BF16)] * 2,
        in_specs=[pl.BlockSpec(memory_space=pltpu.HBM)] * 4,
        out_specs=[pl.BlockSpec(memory_space=pltpu.VMEM)] * 2,
        scratch_shapes=[
            vmem((4, ROWS, COLS), BF16),
            vmem((4, ROWS, COLS), BF16),
            vmem((4, ROWS, COLS), BF16),
            vmem((2, 4, ROWS, COLS), BF16),
            vmem((ROWS, COLS), BF16),
            vmem((4, 2, COLS, COLS), BF16),
            vmem((ROWS, COLS), BF16),
            vmem((1, COLS), F32),
            vmem((2, 4, 1, COLS), F32),
            vmem((2, 1, COLS), F32),
            vmem((16, 2, 1, COLS), F32),
            vmem((1, COLS), F32),
            vmem((16, 1, COLS), F32),
            vmem((2, 2, 8, UNIT, COLS), F32),
            vmem((2, 2, 2, 4, UNIT, COLS), BF16),
            vmem((2, 2, 2, 4, UNIT, COLS), BF16),
            vmem((2, 2, UNIT, COLS), BF16),
            vmem((2, 2, UNIT, COLS), BF16),
            vmem((2, 2, 8, UNIT, COLS), BF16),
            vmem((2, 4, ROWS, COLS // 2), F32),
            vmem((2, 4, ROWS, COLS // 2), BF16),
            vmem((2, 4, ROWS, COLS // 2), BF16),
            vmem((ROWS, COLS), BF16),
            vmem((4, ROWS, COLS), BF16),
            vmem((4, ROWS, COLS), BF16),
            vmem((ROWS, COLS), F32),
            dma((5,)),
            dma((4,)), dma((4,)), dma((4,)), dma((4,)),
            dma((2, 4)), dma((2, 4)), dma((16,)), dma((16,)), dma((16,)), dma((16,)),
            dma, dma, dma((2, 2, 2, 4)), dma((2, 2, 2, 4)), dma((2, 2)), dma((2, 2)),
            dma((2, 2, 2, 4)), dma((2, 2, 2, 4)),
            dma((2, 4)), dma((2, 4)), dma((2,)), dma((2,)), dma((4,)), dma((4,)),
            dma((4,)), dma((4,)), dma((4,)),
        ],
        compiler_params=pltpu.CompilerParams(
            collective_id=0, has_side_effects=True, vmem_limit_bytes=60 * 2**20),
        cost_estimate=pl.CostEstimate(flops=2700000000, bytes_accessed=5000000, transcendentals=0),
        name="vicreg_backward",
    )(first_view, second_view, weight.reshape(8, COLS, COLS), pre_act)


def store_kernel(a, b, a_out, b_out):
    a_out[...] = a[...]
    b_out[...] = b[...]


def on_device(*args):
    return pl.pallas_call(
        store_kernel,
        out_shape=[jax.ShapeDtypeStruct((ROWS, COLS), BF16)] * 2,
        in_specs=[pl.BlockSpec(memory_space=pltpu.VMEM)] * 2,
        out_specs=[pl.BlockSpec(memory_space=pltpu.VMEM)] * 2,
        compiler_params=pltpu.CompilerParams(vmem_limit_bytes=60 * 2**20),
        name="store",
    )(*backward(*args))


def solution(mesh):
    return jax.shard_map(
        on_device,
        mesh=mesh,
        in_specs=(P("pairs", "dims"), P("pairs", "dims"), P(None, "dims"), P("pairs", "dims")),
        out_specs=(P("pairs", "dims"), P("pairs", "dims")),
        check_vma=False,
    )
```

```python
import jax
import jax.numpy as jnp
from jax import lax
from jax.experimental import pallas as pl
from jax.experimental.pallas import tpu as pltpu
from jax.sharding import PartitionSpec as P

D = 4096
N = 8192
ROWS = 128
COLS = 512
UNIT = 64
HALF = 256
GROUP = 512

inv_weight = 25.0
var_weight = 25.0
cov_weight = 1.0
var_eps = 1e-05
loss_share = 32.0

F32 = jnp.float32
BF16 = jnp.bfloat16
NT = (((1,), (1,)), ((), ()))
TN = (((0,), (0,)), ((), ()))


def kernel(
    fv, sv, w, pa, vg_out, pg_out,
    xj, xk, pj, pk, svb, wb, pab,
    tot, st, dsj, dsk, dja, dkb, corr,
    cf, rs_s, rs_r, yh_s, yh_r, call,
    cov, cx_s, cx_r, vgp, bk_s, bk_r, keep,
    lsem,
    xj_ss, xj_rs, xk_ss, xk_rs, st_ss, st_rs, dk_ss, dk_rs,
    pk_ss, pk_rs, rsz_ss, rsz_rs, yh_ss, yh_rs, ag_ss, ag_rs,
    cx_ss, cx_rs, vg_ss, vg_rs, bk_ss, bk_rs, w_sem, w_ss, w_rs,
):
    p = lax.axis_index("pairs")
    d = lax.axis_index("dims")
    z, yh, x = p // 8, (p // 4) % 2, p % 4
    yl, c = d // 2, d % 2

    def dev(z_, yh_, x_, yl_, c_):
        return (z_ * 8 + yh_ * 4 + x_, yl_ * 2 + c_)

    def to_x(r):
        return dev(z, yh, (x + r) % 4, yl, c)

    def to_k(r):
        return dev(z, yh, yl, (x + r) % 4, c)

    def from_k(r):
        return dev(z, yh, (yl + 4 - r) % 4, x, c)

    def to_yl(r):
        return dev(z, yh, x, (yl + r) % 4, c)

    def to_zy(r):
        return dev((z + r % 8) % 8, (yh + r // 8) % 2, x, yl, c)

    partner = dev(z, yh, x, yl, 1 - c)
    diagonal = x == yl

    def remote(src, dst, ss, rs, to):
        return pltpu.make_async_remote_copy(
            src_ref=src, dst_ref=dst, send_sem=ss, recv_sem=rs,
            device_id=to, device_id_type=pl.DeviceIdType.MESH)

    cols = (slice(0, HALF), slice(HALF, COLS))

    load_x = pltpu.make_async_copy(fv, xj.at[x], lsem.at[0])
    load_x.start()
    load_w = [
        pltpu.make_async_copy(w.at[i * 2 + c], wb.at[i, 0], w_sem.at[i]) for i in range(4)]
    load_s = pltpu.make_async_copy(sv, svb, lsem.at[2])
    load_p = pltpu.make_async_copy(pa, pab, lsem.at[3])
    load_k = [
        pltpu.make_async_copy(fv.at[:, cols[i]], xk.at[i, x], lsem.at[4 + i]) for i in range(2)]

    barrier = pltpu.get_barrier_semaphore()

    def greet(to):
        pl.semaphore_signal(barrier, inc=1, device_id=to, device_id_type=pl.DeviceIdType.MESH)

    count = 0
    for r in range(1, 16):
        greet(to_zy(r))
        count += 1
    for r in range(1, 4):
        greet(to_x(r))
        greet(to_k(r))
        greet(from_k(r))
        greet(to_yl(r))
        count += 4
    greet(partner)
    count += 1

    @pl.when(jnp.logical_not(diagonal))
    def _():
        greet(to_k(0))
        greet(from_k(0))

    @pl.when(diagonal)
    def _():
        for cp in load_k:
            cp.start()

    for cp in load_w:
        cp.start()
    load_s.start()
    load_p.start()
    load_x.wait()

    @pl.when(jnp.logical_not(diagonal))
    def _():
        pl.semaphore_wait(barrier, count + 2)

    @pl.when(diagonal)
    def _():
        pl.semaphore_wait(barrier, count)

    gj = [remote(xj.at[x], xj.at[x], xj_ss.at[r], xj_rs.at[r], to_x(r)) for r in range(1, 4)]
    gk = [[remote(xj.at[x, :, cols[i]], xk.at[i, x], xk_ss.at[i, r], xk_rs.at[i, r], to_k(r))
           for r in range(4)] for i in range(2)]

    def send_k(i):
        for cp in gk[i][1:]:
            cp.start()

        @pl.when(jnp.logical_not(diagonal))
        def _():
            gk[i][0].start()

    send_k(0)
    for cp in gj:
        cp.start()
    send_k(1)

    lend_w = [
        remote(w.at[i * 2 + 1 - c], wb.at[i, 1], w_ss.at[i], w_rs.at[i], partner) for i in range(4)]
    for cp in lend_w:
        cp.start()

    share = []

    def centre_k(i):
        for cp in gk[i][1:]:
            cp.wait_recv()

        @pl.when(jnp.logical_not(diagonal))
        def _():
            gk[i][0].wait_recv()

        @pl.when(diagonal)
        def _():
            load_k[i].wait()

        total = jnp.zeros((1, HALF), F32)
        for b in range(4):
            total = total + jnp.sum(xk[i, b].astype(F32), axis=0, keepdims=True)
        tot[2, :, cols[i]] = total
        for b in range(4):
            pk[0, i, b] = (xk[i, b].astype(F32) - total / GROUP).astype(BF16)
        cp = remote(pk.at[0, i], pk.at[1, i], pk_ss.at[i], pk_rs.at[i], partner)
        cp.start()
        share.append(cp)

    def centre_j():
        for cp in gj:
            cp.wait_recv()
        total = jnp.zeros((1, COLS), F32)
        for b in range(4):
            total = total + jnp.sum(xj[b].astype(F32), axis=0, keepdims=True)
        squares = jnp.zeros((1, COLS), F32)
        for b in range(4):
            centered = xj[b].astype(F32) - total / GROUP
            pj[b] = centered.astype(BF16)
            squares = squares + jnp.sum(centered * centered, axis=0, keepdims=True)
        tot[0] = total
        tot[1] = squares

    def block(i, h):
        prod = lax.dot_general(
            pj[...].reshape(GROUP, COLS), pk[h, i].reshape(GROUP, HALF), TN,
            preferred_element_type=F32)
        cf[i, h] = prod.reshape(8, UNIT, HALF)

    def along(way, hops):
        return dev((z + (hops if way == 0 else 8 - hops)) % 8, yh, x, yl, c)

    def unit(way, hops):
        return (z + (hops if way == 0 else 8 - hops)) % 8

    sent = []
    rs = {}

    def reduce_step(i, h, way, k):
        if k == 4 and h != way:
            return
        val = cf[i, h, unit(way, k)]
        for m in {2: (4, 3), 1: (2,)}.get(k, ()):
            if (i, h, way, m) in rs:
                rs[i, h, way, m].wait_recv()
                val = val + rs_r[i, h, way, m - 1].astype(F32)
        at = (i, h, way, k - 1)
        rs_s[at] = val.astype(BF16)
        cp = remote(rs_s.at[at], rs_r.at[at], rsz_ss.at[at], rsz_rs.at[at],
                    along(way, 2 if k == 4 else 1))
        cp.start()
        rs[i, h, way, k] = cp
        sent.append(cp)

    def start_reduce(i, h):
        for way in range(2):
            reduce_step(i, h, way, 4)
            reduce_step(i, h, way, 3)

    def reduce_all(i, k):
        for h in range(2):
            for way in range(2):
                reduce_step(i, h, way, k)

    swap = {}

    def swap_out(i):
        for h in range(2):
            mine = cf[i, h, z]
            for way in range(2):
                rs[i, h, way, 1].wait_recv()
                mine = mine + rs_r[i, h, way, 0].astype(F32)
            cf[i, h, z] = mine
            yh_s[i, h] = mine.astype(BF16)
            cp = remote(yh_s.at[i, h], yh_r.at[i, h], yh_ss.at[i, h], yh_rs.at[i, h], to_zy(8))
            cp.start()
            swap[i, h] = cp
            sent.append(cp)

    ag = {}

    def gather_step(i, h, way, k):
        if k == 4 and h != way:
            return
        if k > 1 and k != 4:
            ag[i, h, way, k - 1].wait_recv()
        at = (i, h, way, k - 1)
        held = call.at[i, h, unit(1 - way, min(k, 3) - 1)]
        cp = remote(held, held, ag_ss.at[at], ag_rs.at[at], along(way, 2 if k == 4 else 1))
        cp.start()
        ag[i, h, way, k] = cp
        sent.append(cp)

    def gather_first(i):
        for h in range(2):
            swap[i, h].wait_recv()
            full = cf[i, h, z] + yh_r[i, h].astype(F32) + corr[h, z, :, cols[i]]
            call[i, h, z] = full.astype(BF16)
            for way in range(2):
                gather_step(i, h, way, 1)

    def gather_all(i, k):
        for h in range(2):
            for way in range(2):
                gather_step(i, h, way, k)
                if k == 3:
                    gather_step(i, h, way, 4)

    def gather_wait(i):
        for h in range(2):
            for way in range(2):
                ag[i, h, way, 3].wait_recv()
            ag[i, h, h, 4].wait_recv()

    centre_k(0)
    centre_j()
    block(0, 0)
    start_reduce(0, 0)
    share[0].wait_recv()
    block(0, 1)
    start_reduce(0, 1)
    centre_k(1)
    block(1, 0)
    start_reduce(1, 0)
    share[1].wait_recv()
    block(1, 1)
    start_reduce(1, 1)

    s2 = [remote(tot, st.at[r], st_ss.at[r], st_rs.at[r], to_zy(r)) for r in range(1, 16)]
    for cp in s2:
        cp.start()
    reduce_all(0, 2)
    reduce_all(0, 1)
    reduce_all(1, 2)
    swap_out(0)
    reduce_all(1, 1)

    for cp in s2:
        cp.wait_recv()
    sums = tot[...]
    for r in range(1, 16):
        sums = sums + st[r]
    mean_j, mean_k = sums[0] / N, sums[2] / N
    for r in range(16):
        own = tot[...] if r == 0 else st[r]
        dsj[r:r + 1, :] = own[0] / GROUP - mean_j
        dsk[r:r + 1, :] = own[2] / GROUP - mean_k
    gap_j, gap_k = dsj[...], dsk[...]
    variance = (sums[1] + GROUP * jnp.sum(gap_j * gap_j, axis=0, keepdims=True)) / (N - 1)
    deviation = jnp.sqrt(variance + var_eps)
    hinge = jnp.where(deviation < 1.0, 1.0, 0.0).astype(F32)

    def split(value):
        high = value.astype(BF16)
        return high, (value - high.astype(F32)).astype(BF16)

    high, low = split(GROUP * gap_j)
    dja[0:16], dja[16:32], dja[32:48] = high, high, low
    high, low = split(gap_k)
    dkb[0, 0:16], dkb[0, 16:32], dkb[0, 32:48] = high, low, high
    share_d = remote(dkb.at[0], dkb.at[1], dk_ss, dk_rs, partner)
    share_d.start()

    def correction(h):
        corr[h] = lax.dot_general(
            dja[...], dkb[h], TN, preferred_element_type=F32).reshape(8, UNIT, COLS)

    correction(0)
    swap_out(1)
    share_d.wait_recv()
    correction(1)
    gather_first(0)

    for i in range(2):
        share[i].wait_send()
        for h in range(2):
            shift = dkb[h, 0:16].astype(F32)[0:1] + dkb[h, 16:32].astype(F32)[0:1]
            for b in range(4):
                pk[h, i, b] = (pk[h, i, b].astype(F32) + shift[:, cols[i]]).astype(BF16)
    gather_all(0, 2)
    gather_first(1)
    gather_all(0, 3)
    gather_all(1, 2)
    gather_all(1, 3)

    cx = {}

    def product(i, q):
        out = None
        for h in range(2):
            part = lax.dot_general(
                pk[h, i].reshape(GROUP, HALF), call[i, h, 4 * q:4 * q + 4].reshape(HALF, HALF), NT,
                preferred_element_type=F32)
            out = part if out is None else out + part
        return out.reshape(4, ROWS, HALF)

    gather_wait(0)
    for q in range(2):
        cov[q] = product(0, q)
    gather_wait(1)
    for q in range(2):
        cov[q] += product(1, q)
        for r in (2, 1, 3):
            cx_s[q, r] = cov[q, (x + r) % 4].astype(BF16)
            cp = remote(cx_s.at[q, r], cx_r.at[q, r], cx_ss.at[q, r], cx_rs.at[q, r], to_x(r))
            cp.start()
            cx[q, r] = cp
            sent.append(cp)

    load_s.wait()
    factor = N * D / loss_share
    vgc = []

    def view_grad(q):
        at = slice(q * HALF, (q + 1) * HALF)
        cov_prod = cov[q, x]
        for r in range(1, 4):
            cx[q, r].wait_recv()
            cov_prod = cov_prod + cx_r[q, r].astype(F32)
        values = xj[x, :, at].astype(F32)
        centered = values - mean_j[:, at]
        invariance = 2.0 * inv_weight / (N * D) * (values - svb[:, at].astype(F32))
        spread_term = -var_weight / D * hinge[:, at] * centered / ((N - 1) * deviation[:, at])
        cov_term = 4.0 * cov_weight / (D * (N - 1)) * (cov_prod / (N - 1) - centered * variance[:, at])
        vg_out[:, at] = (factor * (invariance + spread_term + cov_term)).astype(BF16)
        cp = remote(vg_out.at[:, at], vgp.at[:, at], vg_ss.at[q], vg_rs.at[q], partner)
        cp.start()
        vgc.append(cp)
        sent.append(cp)

    view_grad(0)
    view_grad(1)

    bk = []

    def back(r):
        at = (yl + r) % 4
        out = lax.dot_general(vg_out[...], wb[at, 0], NT, preferred_element_type=F32)
        if r == 2:
            for cp in vgc:
                cp.wait_recv()
        return out + lax.dot_general(vgp[...], wb[at, 1], NT, preferred_element_type=F32)

    for cp in load_w:
        cp.wait()
    for cp in lend_w:
        cp.wait_recv()
    for r in (2, 1, 3):
        bk_s[r] = back(r).astype(BF16)
        cp = remote(bk_s.at[r], bk_r.at[r], bk_ss.at[r], bk_rs.at[r], to_yl(r))
        cp.start()
        bk.append(cp)
        sent.append(cp)
    keep[...] = back(0)
    load_p.wait()
    for cp in bk:
        cp.wait_recv()
    total = keep[...]
    for r in range(1, 4):
        total = total + bk_r[r].astype(F32)
    pg_out[...] = jnp.where(pab[...] > 0, total, 0.0).astype(BF16)

    for cp in gj + gk[0][1:] + gk[1][1:] + s2 + [share_d] + lend_w + sent:
        cp.wait_send()

    @pl.when(jnp.logical_not(diagonal))
    def _():
        gk[0][0].wait_send()
        gk[1][0].wait_send()


def backward(first_view, second_view, weight, pre_act):
    dma = pltpu.SemaphoreType.DMA
    vmem = pltpu.VMEM
    return pl.pallas_call(
        kernel,
        out_shape=[jax.ShapeDtypeStruct((ROWS, COLS), BF16)] * 2,
        in_specs=[pl.BlockSpec(memory_space=pltpu.HBM)] * 4,
        out_specs=[pl.BlockSpec(memory_space=pltpu.VMEM)] * 2,
        scratch_shapes=[
            vmem((4, ROWS, COLS), BF16),
            vmem((2, 4, ROWS, HALF), BF16),
            vmem((4, ROWS, COLS), BF16),
            vmem((2, 2, 4, ROWS, HALF), BF16),
            vmem((ROWS, COLS), BF16),
            vmem((4, 2, COLS, COLS), BF16),
            vmem((ROWS, COLS), BF16),
            vmem((3, 1, COLS), F32),
            vmem((16, 3, 1, COLS), F32),
            vmem((16, COLS), F32),
            vmem((16, COLS), F32),
            vmem((48, COLS), BF16),
            vmem((2, 48, COLS), BF16),
            vmem((2, 8, UNIT, COLS), F32),
            vmem((2, 2, 8, UNIT, HALF), F32),
            vmem((2, 2, 2, 4, UNIT, HALF), BF16),
            vmem((2, 2, 2, 4, UNIT, HALF), BF16),
            vmem((2, 2, UNIT, HALF), BF16),
            vmem((2, 2, UNIT, HALF), BF16),
            vmem((2, 2, 8, UNIT, HALF), BF16),
            vmem((2, 4, ROWS, HALF), F32),
            vmem((2, 4, ROWS, HALF), BF16),
            vmem((2, 4, ROWS, HALF), BF16),
            vmem((ROWS, COLS), BF16),
            vmem((4, ROWS, COLS), BF16),
            vmem((4, ROWS, COLS), BF16),
            vmem((ROWS, COLS), F32),
            dma((6,)),
            dma((4,)), dma((4,)), dma((2, 4)), dma((2, 4)), dma((16,)), dma((16,)), dma, dma,
            dma((2,)), dma((2,)), dma((2, 2, 2, 4)), dma((2, 2, 2, 4)), dma((2, 2)), dma((2, 2)),
            dma((2, 2, 2, 4)), dma((2, 2, 2, 4)),
            dma((2, 4)), dma((2, 4)), dma((2,)), dma((2,)), dma((4,)), dma((4,)),
            dma((4,)), dma((4,)), dma((4,)),
        ],
        compiler_params=pltpu.CompilerParams(
            collective_id=0, has_side_effects=True, vmem_limit_bytes=60 * 2**20),
        cost_estimate=pl.CostEstimate(flops=2700000000, bytes_accessed=5000000, transcendentals=0),
        name="vicreg_backward",
    )(first_view, second_view, weight.reshape(8, COLS, COLS), pre_act)


def store_kernel(a, b, a_out, b_out):
    a_out[...] = a[...]
    b_out[...] = b[...]


def on_device(*args):
    return pl.pallas_call(
        store_kernel,
        out_shape=[jax.ShapeDtypeStruct((ROWS, COLS), BF16)] * 2,
        in_specs=[pl.BlockSpec(memory_space=pltpu.VMEM)] * 2,
        out_specs=[pl.BlockSpec(memory_space=pltpu.VMEM)] * 2,
        compiler_params=pltpu.CompilerParams(vmem_limit_bytes=60 * 2**20),
        name="store",
    )(*backward(*args))


def solution(mesh):
    return jax.shard_map(
        on_device,
        mesh=mesh,
        in_specs=(P("pairs", "dims"), P("pairs", "dims"), P(None, "dims"), P("pairs", "dims")),
        out_specs=(P("pairs", "dims"), P("pairs", "dims")),
        check_vma=False,
    )
```

```python
import jax
import jax.numpy as jnp
from jax import lax
from jax.experimental import pallas as pl
from jax.experimental.pallas import tpu as pltpu
from jax.sharding import PartitionSpec as P

D = 4096
N = 8192
ROWS = 128
COLS = 512
UNIT = 64
HALF = 256
GROUP = 512

inv_weight = 25.0
var_weight = 25.0
cov_weight = 1.0
var_eps = 1e-05
loss_share = 32.0

F32 = jnp.float32
BF16 = jnp.bfloat16
NT = (((1,), (1,)), ((), ()))
TN = (((0,), (0,)), ((), ()))


def kernel(
    fv, sv, w, pa, vg_out, pg_out,
    xj, xk, pj, pk, svb, wb, pab,
    tot, st, dsj, dsk, dja, dkb, corr,
    cf, rs_s, rs_r, yh_s, yh_r, call,
    cov, cx_s, cx_r, vgp, bk_s, bk_r, keep,
    lsem,
    xj_ss, xj_rs, xk_ss, xk_rs, st_ss, st_rs, dk_ss, dk_rs,
    pk_ss, pk_rs, rsz_ss, rsz_rs, yh_ss, yh_rs, ag_ss, ag_rs,
    cx_ss, cx_rs, vg_ss, vg_rs, bk_ss, bk_rs, w_sem, w_ss, w_rs,
):
    p = lax.axis_index("pairs")
    d = lax.axis_index("dims")
    z, yh, x = p // 8, (p // 4) % 2, p % 4
    yl, c = d // 2, d % 2

    def dev(z_, yh_, x_, yl_, c_):
        return (z_ * 8 + yh_ * 4 + x_, yl_ * 2 + c_)

    def to_x(r):
        return dev(z, yh, (x + r) % 4, yl, c)

    def to_k(r):
        return dev(z, yh, yl, (x + r) % 4, c)

    def from_k(r):
        return dev(z, yh, (yl + 4 - r) % 4, x, c)

    def to_yl(r):
        return dev(z, yh, x, (yl + r) % 4, c)

    def to_zy(r):
        return dev((z + r % 8) % 8, (yh + r // 8) % 2, x, yl, c)

    partner = dev(z, yh, x, yl, 1 - c)
    diagonal = x == yl

    def remote(src, dst, ss, rs, to):
        return pltpu.make_async_remote_copy(
            src_ref=src, dst_ref=dst, send_sem=ss, recv_sem=rs,
            device_id=to, device_id_type=pl.DeviceIdType.MESH)

    cols = (slice(0, HALF), slice(HALF, COLS))

    load_x = pltpu.make_async_copy(fv, xj.at[x], lsem.at[0])
    load_x.start()
    load_w = [
        pltpu.make_async_copy(w.at[i * 2 + c], wb.at[i, 0], w_sem.at[i]) for i in range(4)]
    load_s = pltpu.make_async_copy(sv, svb, lsem.at[2])
    load_p = pltpu.make_async_copy(pa, pab, lsem.at[3])
    load_k = [
        pltpu.make_async_copy(fv.at[:, cols[i]], xk.at[i, x], lsem.at[4 + i]) for i in range(2)]

    barrier = pltpu.get_barrier_semaphore()

    def greet(to):
        pl.semaphore_signal(barrier, inc=1, device_id=to, device_id_type=pl.DeviceIdType.MESH)

    count = 0
    for r in range(1, 16):
        greet(to_zy(r))
        count += 1
    for r in range(1, 4):
        greet(to_x(r))
        greet(to_k(r))
        greet(from_k(r))
        greet(to_yl(r))
        count += 4
    greet(partner)
    count += 1

    @pl.when(jnp.logical_not(diagonal))
    def _():
        greet(to_k(0))
        greet(from_k(0))

    @pl.when(diagonal)
    def _():
        for cp in load_k:
            cp.start()

    for cp in load_w:
        cp.start()
    load_s.start()
    load_p.start()
    load_x.wait()

    @pl.when(jnp.logical_not(diagonal))
    def _():
        pl.semaphore_wait(barrier, count + 2)

    @pl.when(diagonal)
    def _():
        pl.semaphore_wait(barrier, count)

    gj = [remote(xj.at[x], xj.at[x], xj_ss.at[r], xj_rs.at[r], to_x(r)) for r in range(1, 4)]
    gk = [[remote(xj.at[x, :, cols[i]], xk.at[i, x], xk_ss.at[i, r], xk_rs.at[i, r], to_k(r))
           for r in range(4)] for i in range(2)]

    def send_k(i):
        for cp in gk[i][1:]:
            cp.start()

        @pl.when(jnp.logical_not(diagonal))
        def _():
            gk[i][0].start()

    send_k(0)
    for cp in gj:
        cp.start()
    send_k(1)

    lend_w = [
        remote(w.at[i * 2 + 1 - c], wb.at[i, 1], w_ss.at[i], w_rs.at[i], partner) for i in range(4)]
    for cp in lend_w:
        cp.start()

    share = []

    def centre_k(i):
        for cp in gk[i][1:]:
            cp.wait_recv()

        @pl.when(jnp.logical_not(diagonal))
        def _():
            gk[i][0].wait_recv()

        @pl.when(diagonal)
        def _():
            load_k[i].wait()

        total = jnp.zeros((1, HALF), F32)
        for b in range(4):
            total = total + jnp.sum(xk[i, b].astype(F32), axis=0, keepdims=True)
        tot[2, :, cols[i]] = total
        for b in range(4):
            pk[0, i, b] = (xk[i, b].astype(F32) - total / GROUP).astype(BF16)
        cp = remote(pk.at[0, i], pk.at[1, i], pk_ss.at[i], pk_rs.at[i], partner)
        cp.start()
        share.append(cp)

    def centre_j():
        for cp in gj:
            cp.wait_recv()
        total = jnp.zeros((1, COLS), F32)
        for b in range(4):
            total = total + jnp.sum(xj[b].astype(F32), axis=0, keepdims=True)
        squares = jnp.zeros((1, COLS), F32)
        for b in range(4):
            centered = xj[b].astype(F32) - total / GROUP
            pj[b] = centered.astype(BF16)
            squares = squares + jnp.sum(centered * centered, axis=0, keepdims=True)
        tot[0] = total
        tot[1] = squares

    def block(i, h):
        prod = lax.dot_general(
            pj[...].reshape(GROUP, COLS), pk[h, i].reshape(GROUP, HALF), TN,
            preferred_element_type=F32)
        cf[i, :, h] = prod.reshape(8, UNIT, HALF)

    def along(way, hops):
        return dev((z + (hops if way == 0 else 8 - hops)) % 8, yh, x, yl, c)

    def unit(way, hops):
        return (z + (hops if way == 0 else 8 - hops)) % 8

    sent = []
    rs = {}

    def reduce_step(i, way, k):
        at = unit(way, k)
        if k == 4:
            held, land = rs_s.at[i, way, 3, way], rs_r.at[i, way, 3, way]
            rs_s[i, way, 3, way] = cf[i, at, way].astype(BF16)
        else:
            held, land = rs_s.at[i, way, k - 1], rs_r.at[i, way, k - 1]
            if k == 2:
                rs[i, way, 4].wait_recv()
            if k < 3:
                rs[i, way, k + 1].wait_recv()
            for h in range(2):
                val = cf[i, at, h]
                if k == 2 and h == way:
                    val = val + rs_r[i, way, 3, h].astype(F32)
                if k < 3:
                    val = val + rs_r[i, way, k, h].astype(F32)
                rs_s[i, way, k - 1, h] = val.astype(BF16)
        cp = remote(held, land, rsz_ss.at[i, way, k - 1], rsz_rs.at[i, way, k - 1],
                    along(way, 2 if k == 4 else 1))
        cp.start()
        rs[i, way, k] = cp
        sent.append(cp)

    def reduce_all(i, *steps):
        for k in steps:
            for way in range(2):
                reduce_step(i, way, k)

    swap = {}

    def swap_out(i):
        for way in range(2):
            rs[i, way, 1].wait_recv()
        for h in range(2):
            mine = cf[i, z, h] + rs_r[i, 0, 0, h].astype(F32) + rs_r[i, 1, 0, h].astype(F32)
            cf[i, z, h] = mine
            yh_s[i, h] = mine.astype(BF16)
        cp = remote(yh_s.at[i], yh_r.at[i], yh_ss.at[i], yh_rs.at[i], to_zy(8))
        cp.start()
        swap[i] = cp
        sent.append(cp)

    ag = {}

    def gather_step(i, way, k):
        if k in (2, 4):
            ag[i, way, k // 2].wait_recv()
        held = call.at[i, unit(1 - way, min(k, 3) - 1)]
        if k == 4:
            held = call.at[i, unit(1 - way, 2), way]
        cp = remote(held, held, ag_ss.at[i, way, k - 1], ag_rs.at[i, way, k - 1],
                    along(way, 2 if k == 4 else 1))
        cp.start()
        ag[i, way, k] = cp
        sent.append(cp)

    def gather_first(i):
        swap[i].wait_recv()
        for h in range(2):
            full = cf[i, z, h] + yh_r[i, h].astype(F32) + corr[h, z, :, cols[i]]
            call[i, z, h] = full.astype(BF16)
        gather_all(i, 1)

    def gather_all(i, *steps):
        for k in steps:
            for way in range(2):
                gather_step(i, way, k)

    def gather_wait(i):
        for way in range(2):
            ag[i, way, 3].wait_recv()
            ag[i, way, 4].wait_recv()

    centre_k(0)
    centre_j()
    block(0, 0)
    share[0].wait_recv()
    block(0, 1)
    reduce_all(0, 4, 3)
    centre_k(1)
    block(1, 0)
    share[1].wait_recv()
    block(1, 1)
    reduce_all(1, 4, 3)
    reduce_all(0, 2)

    s2 = [remote(tot, st.at[r], st_ss.at[r], st_rs.at[r], to_zy(r)) for r in range(1, 16)]
    for cp in s2:
        cp.start()
    reduce_all(0, 1)
    reduce_all(1, 2)
    swap_out(0)
    reduce_all(1, 1)

    for cp in s2:
        cp.wait_recv()
    sums = tot[...]
    for r in range(1, 16):
        sums = sums + st[r]
    mean_j, mean_k = sums[0] / N, sums[2] / N
    for r in range(16):
        own = tot[...] if r == 0 else st[r]
        dsj[r:r + 1, :] = own[0] / GROUP - mean_j
        dsk[r:r + 1, :] = own[2] / GROUP - mean_k
    gap_j, gap_k = dsj[...], dsk[...]
    variance = (sums[1] + GROUP * jnp.sum(gap_j * gap_j, axis=0, keepdims=True)) / (N - 1)
    deviation = jnp.sqrt(variance + var_eps)
    hinge = jnp.where(deviation < 1.0, 1.0, 0.0).astype(F32)

    def split(value):
        high = value.astype(BF16)
        return high, (value - high.astype(F32)).astype(BF16)

    high, low = split(GROUP * gap_j)
    dja[0:16], dja[16:32], dja[32:48] = high, high, low
    high, low = split(gap_k)
    dkb[0, 0:16], dkb[0, 16:32], dkb[0, 32:48] = high, low, high
    share_d = remote(dkb.at[0], dkb.at[1], dk_ss, dk_rs, partner)
    share_d.start()

    def correction(h):
        corr[h] = lax.dot_general(
            dja[...], dkb[h], TN, preferred_element_type=F32).reshape(8, UNIT, COLS)

    correction(0)
    swap_out(1)
    share_d.wait_recv()
    correction(1)
    gather_first(0)

    for i in range(2):
        share[i].wait_send()
        for h in range(2):
            shift = dkb[h, 0:16].astype(F32)[0:1] + dkb[h, 16:32].astype(F32)[0:1]
            for b in range(4):
                pk[h, i, b] = (pk[h, i, b].astype(F32) + shift[:, cols[i]]).astype(BF16)
    gather_all(0, 2)
    gather_first(1)
    gather_all(0, 4, 3)
    gather_all(1, 2)
    gather_all(1, 4, 3)

    cx = {}

    def product(i, q):
        out = None
        for h in range(2):
            part = lax.dot_general(
                pk[h, i].reshape(GROUP, HALF), call[i, 4 * q:4 * q + 4, h].reshape(HALF, HALF), NT,
                preferred_element_type=F32)
            out = part if out is None else out + part
        return out.reshape(4, ROWS, HALF)

    gather_wait(0)
    for q in range(2):
        cov[q] = product(0, q)
    gather_wait(1)
    for q in range(2):
        cov[q] += product(1, q)
        for r in (2, 1, 3):
            cx_s[q, r] = cov[q, (x + r) % 4].astype(BF16)
            cp = remote(cx_s.at[q, r], cx_r.at[q, r], cx_ss.at[q, r], cx_rs.at[q, r], to_x(r))
            cp.start()
            cx[q, r] = cp
            sent.append(cp)

    load_s.wait()
    factor = N * D / loss_share
    vgc = []

    def view_grad(q):
        at = slice(q * HALF, (q + 1) * HALF)
        cov_prod = cov[q, x]
        for r in range(1, 4):
            cx[q, r].wait_recv()
            cov_prod = cov_prod + cx_r[q, r].astype(F32)
        values = xj[x, :, at].astype(F32)
        centered = values - mean_j[:, at]
        invariance = 2.0 * inv_weight / (N * D) * (values - svb[:, at].astype(F32))
        spread_term = -var_weight / D * hinge[:, at] * centered / ((N - 1) * deviation[:, at])
        cov_term = 4.0 * cov_weight / (D * (N - 1)) * (cov_prod / (N - 1) - centered * variance[:, at])
        vg_out[:, at] = (factor * (invariance + spread_term + cov_term)).astype(BF16)
        cp = remote(vg_out.at[:, at], vgp.at[:, at], vg_ss.at[q], vg_rs.at[q], partner)
        cp.start()
        vgc.append(cp)
        sent.append(cp)

    view_grad(0)
    view_grad(1)

    bk = []

    def back(r):
        at = (yl + r) % 4
        out = lax.dot_general(vg_out[...], wb[at, 0], NT, preferred_element_type=F32)
        if r == 2:
            for cp in vgc:
                cp.wait_recv()
        return out + lax.dot_general(vgp[...], wb[at, 1], NT, preferred_element_type=F32)

    for cp in load_w:
        cp.wait()
    for cp in lend_w:
        cp.wait_recv()
    for r in (2, 1, 3):
        bk_s[r] = back(r).astype(BF16)
        cp = remote(bk_s.at[r], bk_r.at[r], bk_ss.at[r], bk_rs.at[r], to_yl(r))
        cp.start()
        bk.append(cp)
        sent.append(cp)
    keep[...] = back(0)
    load_p.wait()
    for cp in bk:
        cp.wait_recv()
    total = keep[...]
    for r in range(1, 4):
        total = total + bk_r[r].astype(F32)
    pg_out[...] = jnp.where(pab[...] > 0, total, 0.0).astype(BF16)

    for cp in gj + gk[0][1:] + gk[1][1:] + s2 + [share_d] + lend_w + sent:
        cp.wait_send()

    @pl.when(jnp.logical_not(diagonal))
    def _():
        gk[0][0].wait_send()
        gk[1][0].wait_send()


def backward(first_view, second_view, weight, pre_act):
    dma = pltpu.SemaphoreType.DMA
    vmem = pltpu.VMEM
    return pl.pallas_call(
        kernel,
        out_shape=[jax.ShapeDtypeStruct((ROWS, COLS), BF16)] * 2,
        in_specs=[pl.BlockSpec(memory_space=pltpu.HBM)] * 4,
        out_specs=[pl.BlockSpec(memory_space=pltpu.VMEM)] * 2,
        scratch_shapes=[
            vmem((4, ROWS, COLS), BF16),
            vmem((2, 4, ROWS, HALF), BF16),
            vmem((4, ROWS, COLS), BF16),
            vmem((2, 2, 4, ROWS, HALF), BF16),
            vmem((ROWS, COLS), BF16),
            vmem((4, 2, COLS, COLS), BF16),
            vmem((ROWS, COLS), BF16),
            vmem((3, 1, COLS), F32),
            vmem((16, 3, 1, COLS), F32),
            vmem((16, COLS), F32),
            vmem((16, COLS), F32),
            vmem((48, COLS), BF16),
            vmem((2, 48, COLS), BF16),
            vmem((2, 8, UNIT, COLS), F32),
            vmem((2, 8, 2, UNIT, HALF), F32),
            vmem((2, 2, 4, 2, UNIT, HALF), BF16),
            vmem((2, 2, 4, 2, UNIT, HALF), BF16),
            vmem((2, 2, UNIT, HALF), BF16),
            vmem((2, 2, UNIT, HALF), BF16),
            vmem((2, 8, 2, UNIT, HALF), BF16),
            vmem((2, 4, ROWS, HALF), F32),
            vmem((2, 4, ROWS, HALF), BF16),
            vmem((2, 4, ROWS, HALF), BF16),
            vmem((ROWS, COLS), BF16),
            vmem((4, ROWS, COLS), BF16),
            vmem((4, ROWS, COLS), BF16),
            vmem((ROWS, COLS), F32),
            dma((6,)),
            dma((4,)), dma((4,)), dma((2, 4)), dma((2, 4)), dma((16,)), dma((16,)), dma, dma,
            dma((2,)), dma((2,)), dma((2, 2, 4)), dma((2, 2, 4)), dma((2,)), dma((2,)),
            dma((2, 2, 4)), dma((2, 2, 4)),
            dma((2, 4)), dma((2, 4)), dma((2,)), dma((2,)), dma((4,)), dma((4,)),
            dma((4,)), dma((4,)), dma((4,)),
        ],
        compiler_params=pltpu.CompilerParams(
            collective_id=0, has_side_effects=True, vmem_limit_bytes=60 * 2**20),
        cost_estimate=pl.CostEstimate(flops=2700000000, bytes_accessed=5000000, transcendentals=0),
        name="vicreg_backward",
    )(first_view, second_view, weight.reshape(8, COLS, COLS), pre_act)


def store_kernel(a, b, a_out, b_out):
    a_out[...] = a[...]
    b_out[...] = b[...]


def on_device(*args):
    return pl.pallas_call(
        store_kernel,
        out_shape=[jax.ShapeDtypeStruct((ROWS, COLS), BF16)] * 2,
        in_specs=[pl.BlockSpec(memory_space=pltpu.VMEM)] * 2,
        out_specs=[pl.BlockSpec(memory_space=pltpu.VMEM)] * 2,
        compiler_params=pltpu.CompilerParams(vmem_limit_bytes=60 * 2**20),
        name="store",
    )(*backward(*args))


def solution(mesh):
    return jax.shard_map(
        on_device,
        mesh=mesh,
        in_specs=(P("pairs", "dims"), P("pairs", "dims"), P(None, "dims"), P("pairs", "dims")),
        out_specs=(P("pairs", "dims"), P("pairs", "dims")),
        check_vma=False,
    )
```

```python
import jax
import jax.numpy as jnp
from jax import lax
from jax.experimental import pallas as pl
from jax.experimental.pallas import tpu as pltpu
from jax.sharding import PartitionSpec as P

D = 4096
N = 8192
ROWS = 128
COLS = 512
UNIT = 64
HALF = 256
GROUP = 512

inv_weight = 25.0
var_weight = 25.0
cov_weight = 1.0
var_eps = 1e-05
loss_share = 32.0

F32 = jnp.float32
BF16 = jnp.bfloat16
NT = (((1,), (1,)), ((), ()))
TN = (((0,), (0,)), ((), ()))


def kernel(
    fv, sv, w, pa, vg_out, pg_out,
    xj, xk, pj, pk, svb, wb, pab,
    tot, st, dsj, dsk, dja, dkb, corr,
    cf, rs_s, rs_r, yh_s, yh_r, call,
    cov, cx_s, cx_r, vgs, vgp, bk_s, bk_r, keep,
    lsem,
    xj_ss, xj_rs, xk_ss, xk_rs, st_ss, st_rs, dk_ss, dk_rs,
    pk_ss, pk_rs, rsz_ss, rsz_rs, yh_ss, yh_rs, ag_ss, ag_rs,
    cx_ss, cx_rs, vg_ss, vg_rs, bk_ss, bk_rs, w_sem, w_ss, w_rs,
):
    p = lax.axis_index("pairs")
    d = lax.axis_index("dims")
    z, yh, x = p // 8, (p // 4) % 2, p % 4
    yl, c = d // 2, d % 2

    def dev(z_, yh_, x_, yl_, c_):
        return (z_ * 8 + yh_ * 4 + x_, yl_ * 2 + c_)

    def to_x(r):
        return dev(z, yh, (x + r) % 4, yl, c)

    def to_k(r):
        return dev(z, yh, yl, (x + r) % 4, c)

    def from_k(r):
        return dev(z, yh, (yl + 4 - r) % 4, x, c)

    def to_yl(r):
        return dev(z, yh, x, (yl + r) % 4, c)

    def to_zy(r):
        return dev((z + r % 8) % 8, (yh + r // 8) % 2, x, yl, c)

    partner = dev(z, yh, x, yl, 1 - c)
    diagonal = x == yl

    def remote(src, dst, ss, rs, to):
        return pltpu.make_async_remote_copy(
            src_ref=src, dst_ref=dst, send_sem=ss, recv_sem=rs,
            device_id=to, device_id_type=pl.DeviceIdType.MESH)

    cols = (slice(0, HALF), slice(HALF, COLS))

    load_x = pltpu.make_async_copy(fv, xj.at[x], lsem.at[0])
    load_x.start()
    load_w = [
        pltpu.make_async_copy(w.at[i * 2 + c], wb.at[i, 0], w_sem.at[i]) for i in range(4)]
    load_s = pltpu.make_async_copy(sv, svb, lsem.at[2])
    load_p = pltpu.make_async_copy(pa, pab, lsem.at[3])
    load_k = [
        pltpu.make_async_copy(fv.at[:, cols[i]], xk.at[i, x], lsem.at[4 + i]) for i in range(2)]

    barrier = pltpu.get_barrier_semaphore()

    def greet(to):
        pl.semaphore_signal(barrier, inc=1, device_id=to, device_id_type=pl.DeviceIdType.MESH)

    count = 0
    for r in range(1, 16):
        greet(to_zy(r))
        count += 1
    for r in range(1, 4):
        greet(to_x(r))
        greet(to_k(r))
        greet(from_k(r))
        greet(to_yl(r))
        count += 4
    greet(partner)
    count += 1

    @pl.when(jnp.logical_not(diagonal))
    def _():
        greet(to_k(0))
        greet(from_k(0))

    @pl.when(diagonal)
    def _():
        for cp in load_k:
            cp.start()

    for cp in load_w:
        cp.start()
    load_s.start()
    load_p.start()
    load_x.wait()

    @pl.when(jnp.logical_not(diagonal))
    def _():
        pl.semaphore_wait(barrier, count + 2)

    @pl.when(diagonal)
    def _():
        pl.semaphore_wait(barrier, count)

    gj = [remote(xj.at[x], xj.at[x], xj_ss.at[r], xj_rs.at[r], to_x(r)) for r in range(1, 4)]
    gk = [[remote(xj.at[x, :, cols[i]], xk.at[i, x], xk_ss.at[i, r], xk_rs.at[i, r], to_k(r))
           for r in range(4)] for i in range(2)]

    def send_k(i):
        for cp in gk[i][1:]:
            cp.start()

        @pl.when(jnp.logical_not(diagonal))
        def _():
            gk[i][0].start()

    send_k(0)
    for cp in gj:
        cp.start()
    send_k(1)

    lend_w = [
        remote(w.at[i * 2 + 1 - c], wb.at[i, 1], w_ss.at[i], w_rs.at[i], partner) for i in range(4)]
    for cp in lend_w:
        cp.start()

    share = []

    def centre_k(i):
        for cp in gk[i][1:]:
            cp.wait_recv()

        @pl.when(jnp.logical_not(diagonal))
        def _():
            gk[i][0].wait_recv()

        @pl.when(diagonal)
        def _():
            load_k[i].wait()

        total = jnp.zeros((1, HALF), F32)
        for b in range(4):
            total = total + jnp.sum(xk[i, b].astype(F32), axis=0, keepdims=True)
        tot[2, :, cols[i]] = total
        for b in range(4):
            pk[0, i, b] = (xk[i, b].astype(F32) - total / GROUP).astype(BF16)
        cp = remote(pk.at[0, i], pk.at[1, i], pk_ss.at[i], pk_rs.at[i], partner)
        cp.start()
        share.append(cp)

    def centre_j():
        for cp in gj:
            cp.wait_recv()
        total = jnp.zeros((1, COLS), F32)
        for b in range(4):
            total = total + jnp.sum(xj[b].astype(F32), axis=0, keepdims=True)
        squares = jnp.zeros((1, COLS), F32)
        for b in range(4):
            centered = xj[b].astype(F32) - total / GROUP
            pj[b] = centered.astype(BF16)
            squares = squares + jnp.sum(centered * centered, axis=0, keepdims=True)
        tot[0] = total
        tot[1] = squares

    def block(i, h):
        prod = lax.dot_general(
            pj[...].reshape(GROUP, COLS), pk[h, i].reshape(GROUP, HALF), TN,
            preferred_element_type=F32)
        cf[i, :, h] = prod.reshape(8, UNIT, HALF)

    def along(way, hops):
        return dev((z + (hops if way == 0 else 8 - hops)) % 8, yh, x, yl, c)

    def unit(way, hops):
        return (z + (hops if way == 0 else 8 - hops)) % 8

    sent = []
    rs = {}

    def reduce_step(i, way, k):
        at = unit(way, k)
        if k == 4:
            held, land = rs_s.at[i, way, 3, way], rs_r.at[i, way, 3, way]
            rs_s[i, way, 3, way] = cf[i, at, way].astype(BF16)
        else:
            held, land = rs_s.at[i, way, k - 1], rs_r.at[i, way, k - 1]
            if k == 2:
                rs[i, way, 4].wait_recv()
            if k < 3:
                rs[i, way, k + 1].wait_recv()
            for h in range(2):
                val = cf[i, at, h]
                if k == 2 and h == way:
                    val = val + rs_r[i, way, 3, h].astype(F32)
                if k < 3:
                    val = val + rs_r[i, way, k, h].astype(F32)
                rs_s[i, way, k - 1, h] = val.astype(BF16)
        cp = remote(held, land, rsz_ss.at[i, way, k - 1], rsz_rs.at[i, way, k - 1],
                    along(way, 2 if k == 4 else 1))
        cp.start()
        rs[i, way, k] = cp
        sent.append(cp)

    def reduce_all(i, *steps):
        for k in steps:
            for way in range(2):
                reduce_step(i, way, k)

    swap = {}

    def swap_out(i):
        for way in range(2):
            rs[i, way, 1].wait_recv()
        for h in range(2):
            mine = cf[i, z, h] + rs_r[i, 0, 0, h].astype(F32) + rs_r[i, 1, 0, h].astype(F32)
            cf[i, z, h] = mine
            yh_s[i, h] = mine.astype(BF16)
        cp = remote(yh_s.at[i], yh_r.at[i], yh_ss.at[i], yh_rs.at[i], to_zy(8))
        cp.start()
        swap[i] = cp
        sent.append(cp)

    ag = {}

    def gather_step(i, way, k):
        if k in (2, 4):
            ag[i, way, k // 2].wait_recv()
        held = call.at[i, unit(1 - way, min(k, 3) - 1)]
        if k == 4:
            held = call.at[i, unit(1 - way, 2), way]
        cp = remote(held, held, ag_ss.at[i, way, k - 1], ag_rs.at[i, way, k - 1],
                    along(way, 2 if k == 4 else 1))
        cp.start()
        ag[i, way, k] = cp
        sent.append(cp)

    def gather_first(i):
        swap[i].wait_recv()
        for h in range(2):
            full = cf[i, z, h] + yh_r[i, h].astype(F32) + corr[h, z, :, cols[i]]
            call[i, z, h] = full.astype(BF16)
        gather_all(i, 1)

    def gather_all(i, *steps):
        for k in steps:
            for way in range(2):
                gather_step(i, way, k)

    def gather_wait(i):
        for way in range(2):
            ag[i, way, 3].wait_recv()
            ag[i, way, 4].wait_recv()

    centre_k(0)
    centre_j()
    block(0, 0)
    share[0].wait_recv()
    block(0, 1)
    reduce_all(0, 4, 3)
    centre_k(1)

    s2 = [remote(tot, st.at[r], st_ss.at[r], st_rs.at[r], to_zy(r)) for r in range(1, 16)]
    for cp in s2:
        cp.start()
    block(1, 0)
    share[1].wait_recv()
    block(1, 1)
    reduce_all(1, 4, 3)
    reduce_all(0, 2)
    reduce_all(0, 1)
    reduce_all(1, 2)
    swap_out(0)
    reduce_all(1, 1)

    for cp in s2:
        cp.wait_recv()
    sums = tot[...]
    for r in range(1, 16):
        sums = sums + st[r]
    mean_j, mean_k = sums[0] / N, sums[2] / N
    for r in range(16):
        own = tot[...] if r == 0 else st[r]
        dsj[r:r + 1, :] = own[0] / GROUP - mean_j
        dsk[r:r + 1, :] = own[2] / GROUP - mean_k
    gap_j, gap_k = dsj[...], dsk[...]
    variance = (sums[1] + GROUP * jnp.sum(gap_j * gap_j, axis=0, keepdims=True)) / (N - 1)
    deviation = jnp.sqrt(variance + var_eps)
    hinge = jnp.where(deviation < 1.0, 1.0, 0.0).astype(F32)

    def split(value):
        high = value.astype(BF16)
        return high, (value - high.astype(F32)).astype(BF16)

    high, low = split(GROUP * gap_j)
    dja[0:16], dja[16:32], dja[32:48] = high, high, low
    high, low = split(gap_k)
    dkb[0, 0:16], dkb[0, 16:32], dkb[0, 32:48] = high, low, high
    share_d = remote(dkb.at[0], dkb.at[1], dk_ss, dk_rs, partner)
    share_d.start()

    def correction(h):
        corr[h] = lax.dot_general(
            dja[...], dkb[h], TN, preferred_element_type=F32).reshape(8, UNIT, COLS)

    swap_out(1)
    correction(0)
    share_d.wait_recv()
    correction(1)

    for i in range(2):
        share[i].wait_send()
        for h in range(2):
            shift = dkb[h, 0:16].astype(F32)[0:1] + dkb[h, 16:32].astype(F32)[0:1]
            for b in range(4):
                pk[h, i, b] = (pk[h, i, b].astype(F32) + shift[:, cols[i]]).astype(BF16)
    gather_first(0)
    gather_all(0, 2)
    gather_first(1)
    gather_all(0, 4, 3)
    gather_all(1, 2)
    gather_all(1, 4, 3)

    cx = {}

    def product(i, q):
        out = None
        for h in range(2):
            part = lax.dot_general(
                pk[h, i].reshape(GROUP, HALF), call[i, 4 * q:4 * q + 4, h].reshape(HALF, HALF), NT,
                preferred_element_type=F32)
            out = part if out is None else out + part
        return out.reshape(4, ROWS, HALF)

    gather_wait(0)
    for q in range(2):
        cov[q] = product(0, q)
    gather_wait(1)
    for q in range(2):
        cov[q] += product(1, q)
        for r in (2, 1, 3):
            cx_s[q, r] = cov[q, (x + r) % 4].astype(BF16)
            cp = remote(cx_s.at[q, r], cx_r.at[q, r], cx_ss.at[q, r], cx_rs.at[q, r], to_x(r))
            cp.start()
            cx[q, r] = cp
            sent.append(cp)

    load_s.wait()
    factor = N * D / loss_share
    vgc = []

    def view_grad(q):
        at = slice(q * HALF, (q + 1) * HALF)
        cov_prod = cov[q, x]
        for r in range(1, 4):
            cx[q, r].wait_recv()
            cov_prod = cov_prod + cx_r[q, r].astype(F32)
        values = xj[x, :, at].astype(F32)
        centered = values - mean_j[:, at]
        invariance = 2.0 * inv_weight / (N * D) * (values - svb[:, at].astype(F32))
        spread_term = -var_weight / D * hinge[:, at] * centered / ((N - 1) * deviation[:, at])
        cov_term = 4.0 * cov_weight / (D * (N - 1)) * (cov_prod / (N - 1) - centered * variance[:, at])
        vgs[q] = (factor * (invariance + spread_term + cov_term)).astype(BF16)
        cp = remote(vgs.at[q], vgp.at[q], vg_ss.at[q], vg_rs.at[q], partner)
        cp.start()
        vgc.append(cp)
        sent.append(cp)

    view_grad(0)
    view_grad(1)

    bk = []

    def back(r):
        at = (yl + r) % 4
        out = None
        for core, held in enumerate((vgs, vgp)):
            for q in range(2):
                if core == 1 and r == 2:
                    vgc[q].wait_recv()
                part = lax.dot_general(held[q], wb[at, core, :, cols[q]], NT, preferred_element_type=F32)
                out = part if out is None else out + part
        return out

    for cp in load_w:
        cp.wait()
    for cp in lend_w:
        cp.wait_recv()
    for r in (2, 1, 3):
        bk_s[r] = back(r).astype(BF16)
        cp = remote(bk_s.at[r], bk_r.at[r], bk_ss.at[r], bk_rs.at[r], to_yl(r))
        cp.start()
        bk.append(cp)
        sent.append(cp)
    keep[...] = back(0)
    for q in range(2):
        vg_out[:, cols[q]] = vgs[q]
    load_p.wait()
    for cp in bk:
        cp.wait_recv()
    total = keep[...]
    for r in range(1, 4):
        total = total + bk_r[r].astype(F32)
    pg_out[...] = jnp.where(pab[...] > 0, total, 0.0).astype(BF16)

    for cp in gj + gk[0][1:] + gk[1][1:] + s2 + [share_d] + lend_w + sent:
        cp.wait_send()

    @pl.when(jnp.logical_not(diagonal))
    def _():
        gk[0][0].wait_send()
        gk[1][0].wait_send()


def backward(first_view, second_view, weight, pre_act):
    dma = pltpu.SemaphoreType.DMA
    vmem = pltpu.VMEM
    return pl.pallas_call(
        kernel,
        out_shape=[jax.ShapeDtypeStruct((ROWS, COLS), BF16)] * 2,
        in_specs=[pl.BlockSpec(memory_space=pltpu.HBM)] * 4,
        out_specs=[pl.BlockSpec(memory_space=pltpu.VMEM)] * 2,
        scratch_shapes=[
            vmem((4, ROWS, COLS), BF16),
            vmem((2, 4, ROWS, HALF), BF16),
            vmem((4, ROWS, COLS), BF16),
            vmem((2, 2, 4, ROWS, HALF), BF16),
            vmem((ROWS, COLS), BF16),
            vmem((4, 2, COLS, COLS), BF16),
            vmem((ROWS, COLS), BF16),
            vmem((3, 1, COLS), F32),
            vmem((16, 3, 1, COLS), F32),
            vmem((16, COLS), F32),
            vmem((16, COLS), F32),
            vmem((48, COLS), BF16),
            vmem((2, 48, COLS), BF16),
            vmem((2, 8, UNIT, COLS), F32),
            vmem((2, 8, 2, UNIT, HALF), F32),
            vmem((2, 2, 4, 2, UNIT, HALF), BF16),
            vmem((2, 2, 4, 2, UNIT, HALF), BF16),
            vmem((2, 2, UNIT, HALF), BF16),
            vmem((2, 2, UNIT, HALF), BF16),
            vmem((2, 8, 2, UNIT, HALF), BF16),
            vmem((2, 4, ROWS, HALF), F32),
            vmem((2, 4, ROWS, HALF), BF16),
            vmem((2, 4, ROWS, HALF), BF16),
            vmem((2, ROWS, HALF), BF16),
            vmem((2, ROWS, HALF), BF16),
            vmem((4, ROWS, COLS), BF16),
            vmem((4, ROWS, COLS), BF16),
            vmem((ROWS, COLS), F32),
            dma((6,)),
            dma((4,)), dma((4,)), dma((2, 4)), dma((2, 4)), dma((16,)), dma((16,)), dma, dma,
            dma((2,)), dma((2,)), dma((2, 2, 4)), dma((2, 2, 4)), dma((2,)), dma((2,)),
            dma((2, 2, 4)), dma((2, 2, 4)),
            dma((2, 4)), dma((2, 4)), dma((2,)), dma((2,)), dma((4,)), dma((4,)),
            dma((4,)), dma((4,)), dma((4,)),
        ],
        compiler_params=pltpu.CompilerParams(
            collective_id=0, has_side_effects=True, vmem_limit_bytes=60 * 2**20),
        cost_estimate=pl.CostEstimate(flops=2700000000, bytes_accessed=5000000, transcendentals=0),
        name="vicreg_backward",
    )(first_view, second_view, weight.reshape(8, COLS, COLS), pre_act)


def store_kernel(a, b, a_out, b_out):
    a_out[...] = a[...]
    b_out[...] = b[...]


def on_device(*args):
    return pl.pallas_call(
        store_kernel,
        out_shape=[jax.ShapeDtypeStruct((ROWS, COLS), BF16)] * 2,
        in_specs=[pl.BlockSpec(memory_space=pltpu.VMEM)] * 2,
        out_specs=[pl.BlockSpec(memory_space=pltpu.VMEM)] * 2,
        compiler_params=pltpu.CompilerParams(vmem_limit_bytes=60 * 2**20),
        name="store",
    )(*backward(*args))


def solution(mesh):
    return jax.shard_map(
        on_device,
        mesh=mesh,
        in_specs=(P("pairs", "dims"), P("pairs", "dims"), P(None, "dims"), P("pairs", "dims")),
        out_specs=(P("pairs", "dims"), P("pairs", "dims")),
        check_vma=False,
    )
```

```python
import jax
import jax.numpy as jnp
from jax import lax
from jax.experimental import pallas as pl
from jax.experimental.pallas import tpu as pltpu
from jax.sharding import PartitionSpec as P

D = 4096
N = 8192
ROWS = 128
COLS = 512
UNIT = 64
HALF = 256
GROUP = 512

inv_weight = 25.0
var_weight = 25.0
cov_weight = 1.0
var_eps = 1e-05
loss_share = 32.0

F32 = jnp.float32
BF16 = jnp.bfloat16
NT = (((1,), (1,)), ((), ()))
TN = (((0,), (0,)), ((), ()))


def kernel(
    fv, sv, w, pa, vg_out, pg_out,
    xj, xk, pj, pk, svb, wb, pab,
    tot, st, dsj, dsk, dja, dkb, corr,
    cf, rs_s, rs_r, yh_s, yh_r, call,
    cov, cx_s, cx_r, vgs, vgp, bk_s, bk_r, keep,
    lsem,
    xj_ss, xj_rs, xk_ss, xk_rs, st_ss, st_rs, dk_ss, dk_rs,
    pk_ss, pk_rs, rsz_ss, rsz_rs, yh_ss, yh_rs, ag_ss, ag_rs,
    cx_ss, cx_rs, vg_ss, vg_rs, bk_ss, bk_rs, w_sem, w_ss, w_rs,
):
    p = lax.axis_index("pairs")
    d = lax.axis_index("dims")
    z, yh, x = p // 8, (p // 4) % 2, p % 4
    yl, c = d // 2, d % 2

    def dev(z_, yh_, x_, yl_, c_):
        return (z_ * 8 + yh_ * 4 + x_, yl_ * 2 + c_)

    def to_x(r):
        return dev(z, yh, (x + r) % 4, yl, c)

    def to_k(r):
        return dev(z, yh, yl, (x + r) % 4, c)

    def from_k(r):
        return dev(z, yh, (yl + 4 - r) % 4, x, c)

    def to_yl(r):
        return dev(z, yh, x, (yl + r) % 4, c)

    def to_zy(r):
        return dev((z + r % 8) % 8, (yh + r // 8) % 2, x, yl, c)

    partner = dev(z, yh, x, yl, 1 - c)
    diagonal = x == yl

    def remote(src, dst, ss, rs, to):
        return pltpu.make_async_remote_copy(
            src_ref=src, dst_ref=dst, send_sem=ss, recv_sem=rs,
            device_id=to, device_id_type=pl.DeviceIdType.MESH)

    cols = (slice(0, HALF), slice(HALF, COLS))

    load_x = pltpu.make_async_copy(fv, xj.at[x], lsem.at[0])
    load_x.start()
    load_w = [
        pltpu.make_async_copy(w.at[i * 2 + c], wb.at[i, 0], w_sem.at[i]) for i in range(4)]
    load_s = pltpu.make_async_copy(sv, svb, lsem.at[2])
    load_p = pltpu.make_async_copy(pa, pab, lsem.at[3])
    load_k = [
        pltpu.make_async_copy(fv.at[:, cols[i]], xk.at[i, x], lsem.at[4 + i]) for i in range(2)]

    barrier = pltpu.get_barrier_semaphore()

    def greet(to):
        pl.semaphore_signal(barrier, inc=1, device_id=to, device_id_type=pl.DeviceIdType.MESH)

    count = 0
    for r in range(1, 16):
        greet(to_zy(r))
        count += 1
    for r in range(1, 4):
        greet(to_x(r))
        greet(to_k(r))
        greet(from_k(r))
        greet(to_yl(r))
        count += 4
    greet(partner)
    count += 1

    @pl.when(jnp.logical_not(diagonal))
    def _():
        greet(to_k(0))
        greet(from_k(0))

    @pl.when(diagonal)
    def _():
        for cp in load_k:
            cp.start()

    for cp in load_w:
        cp.start()
    load_s.start()
    load_p.start()
    load_x.wait()

    @pl.when(jnp.logical_not(diagonal))
    def _():
        pl.semaphore_wait(barrier, count + 2)

    @pl.when(diagonal)
    def _():
        pl.semaphore_wait(barrier, count)

    gj = [remote(xj.at[x], xj.at[x], xj_ss.at[r], xj_rs.at[r], to_x(r)) for r in range(1, 4)]
    gk = [[remote(xj.at[x, :, cols[i]], xk.at[i, x], xk_ss.at[i, r], xk_rs.at[i, r], to_k(r))
           for r in range(4)] for i in range(2)]

    def send_k(i):
        for cp in gk[i][1:]:
            cp.start()

        @pl.when(jnp.logical_not(diagonal))
        def _():
            gk[i][0].start()

    send_k(0)
    for cp in gj:
        cp.start()
    send_k(1)

    lend_w = [
        remote(w.at[i * 2 + 1 - c], wb.at[i, 1], w_ss.at[i], w_rs.at[i], partner) for i in range(4)]
    for cp in lend_w:
        cp.start()

    share = []

    def centre_k(i):
        for cp in gk[i][1:]:
            cp.wait_recv()

        @pl.when(jnp.logical_not(diagonal))
        def _():
            gk[i][0].wait_recv()

        @pl.when(diagonal)
        def _():
            load_k[i].wait()

        total = jnp.zeros((1, HALF), F32)
        for b in range(4):
            total = total + jnp.sum(xk[i, b].astype(F32), axis=0, keepdims=True)
        tot[2, :, cols[i]] = total
        for b in range(4):
            pk[0, i, b] = (xk[i, b].astype(F32) - total / GROUP).astype(BF16)
        cp = remote(pk.at[0, i], pk.at[1, i], pk_ss.at[i], pk_rs.at[i], partner)
        cp.start()
        share.append(cp)

    def centre_j():
        for cp in gj:
            cp.wait_recv()
        total = jnp.zeros((1, COLS), F32)
        for b in range(4):
            total = total + jnp.sum(xj[b].astype(F32), axis=0, keepdims=True)
        squares = jnp.zeros((1, COLS), F32)
        for b in range(4):
            centered = xj[b].astype(F32) - total / GROUP
            pj[b] = centered.astype(BF16)
            squares = squares + jnp.sum(centered * centered, axis=0, keepdims=True)
        tot[0] = total
        tot[1] = squares

    def block(i, h):
        prod = lax.dot_general(
            pj[...].reshape(GROUP, COLS), pk[h, i].reshape(GROUP, HALF), TN,
            preferred_element_type=F32)
        cf[i, :, h] = prod.reshape(8, UNIT, HALF)

    def along(way, hops):
        return dev((z + (hops if way == 0 else 8 - hops)) % 8, yh, x, yl, c)

    def unit(way, hops):
        return (z + (hops if way == 0 else 8 - hops)) % 8

    sent = []
    rs = {}

    def reduce_step(i, way, k):
        at = unit(way, k)
        if k == 4:
            held, land = rs_s.at[i, way, 3, way], rs_r.at[i, way, 3, way]
            rs_s[i, way, 3, way] = cf[i, at, way].astype(BF16)
        else:
            held, land = rs_s.at[i, way, k - 1], rs_r.at[i, way, k - 1]
            if k == 2:
                rs[i, way, 4].wait_recv()
                rs[i, way, 3].wait_recv()
            for h in range(2):
                val = cf[i, at, h]
                if k == 2 and h == way:
                    val = val + rs_r[i, way, 3, h].astype(F32)
                if k == 2:
                    val = val + rs_r[i, way, 2, h].astype(F32)
                rs_s[i, way, k - 1, h] = val.astype(BF16)
        cp = remote(held, land, rsz_ss.at[i, way, k - 1], rsz_rs.at[i, way, k - 1],
                    along(way, 1 if k % 2 else 2))
        cp.start()
        rs[i, way, k] = cp
        sent.append(cp)

    def reduce_all(i, *steps):
        for k in steps:
            for way in range(2):
                reduce_step(i, way, k)

    swap = {}

    def swap_out(i):
        for way in range(2):
            rs[i, way, 1].wait_recv()
            rs[i, way, 2].wait_recv()
        for h in range(2):
            mine = cf[i, z, h]
            for way in range(2):
                mine = mine + rs_r[i, way, 0, h].astype(F32) + rs_r[i, way, 1, h].astype(F32)
            cf[i, z, h] = mine
            yh_s[i, h] = mine.astype(BF16)
        cp = remote(yh_s.at[i], yh_r.at[i], yh_ss.at[i], yh_rs.at[i], to_zy(8))
        cp.start()
        swap[i] = cp
        sent.append(cp)

    ag = {}

    def gather_step(i, way, k):
        if k == 4:
            ag[i, way, 2].wait_recv()
            held = call.at[i, unit(1 - way, 2), way]
        elif k == 3:
            held = call.at[i, unit(1 - way, 2)]
        else:
            held = call.at[i, z]
        cp = remote(held, held, ag_ss.at[i, way, k - 1], ag_rs.at[i, way, k - 1],
                    along(way, 1 if k % 2 else 2))
        cp.start()
        ag[i, way, k] = cp
        sent.append(cp)

    def gather_first(i):
        swap[i].wait_recv()
        for h in range(2):
            full = cf[i, z, h] + yh_r[i, h].astype(F32) + corr[h, z, :, cols[i]]
            call[i, z, h] = full.astype(BF16)
        gather_all(i, 2, 1)

    def gather_all(i, *steps):
        for k in steps:
            for way in range(2):
                gather_step(i, way, k)

    def gather_wait(i):
        for way in range(2):
            ag[i, way, 1].wait_recv()
            ag[i, way, 3].wait_recv()
            ag[i, way, 4].wait_recv()

    centre_k(0)
    centre_j()
    block(0, 0)
    share[0].wait_recv()
    block(0, 1)
    reduce_all(0, 4, 3, 1)
    centre_k(1)

    s2 = [remote(tot, st.at[r], st_ss.at[r], st_rs.at[r], to_zy(r)) for r in range(1, 16)]
    for cp in s2:
        cp.start()
    block(1, 0)
    share[1].wait_recv()
    block(1, 1)
    reduce_all(1, 4, 3, 1)
    reduce_all(0, 2)
    swap_out(0)
    reduce_all(1, 2)

    for cp in s2:
        cp.wait_recv()
    sums = tot[...]
    for r in range(1, 16):
        sums = sums + st[r]
    mean_j, mean_k = sums[0] / N, sums[2] / N
    for r in range(16):
        own = tot[...] if r == 0 else st[r]
        dsj[r:r + 1, :] = own[0] / GROUP - mean_j
        dsk[r:r + 1, :] = own[2] / GROUP - mean_k
    gap_j, gap_k = dsj[...], dsk[...]
    variance = (sums[1] + GROUP * jnp.sum(gap_j * gap_j, axis=0, keepdims=True)) / (N - 1)
    deviation = jnp.sqrt(variance + var_eps)
    hinge = jnp.where(deviation < 1.0, 1.0, 0.0).astype(F32)

    def split(value):
        high = value.astype(BF16)
        return high, (value - high.astype(F32)).astype(BF16)

    high, low = split(GROUP * gap_j)
    dja[0:16], dja[16:32], dja[32:48] = high, high, low
    high, low = split(gap_k)
    dkb[0, 0:16], dkb[0, 16:32], dkb[0, 32:48] = high, low, high
    share_d = remote(dkb.at[0], dkb.at[1], dk_ss, dk_rs, partner)
    share_d.start()

    def correction(h):
        corr[h] = lax.dot_general(
            dja[...], dkb[h], TN, preferred_element_type=F32).reshape(8, UNIT, COLS)

    swap_out(1)
    correction(0)
    share_d.wait_recv()
    correction(1)

    for i in range(2):
        share[i].wait_send()
        for h in range(2):
            shift = dkb[h, 0:16].astype(F32)[0:1] + dkb[h, 16:32].astype(F32)[0:1]
            for b in range(4):
                pk[h, i, b] = (pk[h, i, b].astype(F32) + shift[:, cols[i]]).astype(BF16)
    gather_first(0)
    gather_first(1)
    gather_all(0, 4, 3)
    gather_all(1, 4, 3)

    cx = {}

    def product(i, q):
        out = None
        for h in range(2):
            part = lax.dot_general(
                pk[h, i].reshape(GROUP, HALF), call[i, 4 * q:4 * q + 4, h].reshape(HALF, HALF), NT,
                preferred_element_type=F32)
            out = part if out is None else out + part
        return out.reshape(4, ROWS, HALF)

    gather_wait(0)
    for q in range(2):
        cov[q] = product(0, q)
    gather_wait(1)
    for q in range(2):
        cov[q] += product(1, q)
    halves = (slice(0, ROWS // 2), slice(ROWS // 2, ROWS))
    for i in range(2):
        for r in (2, 1, 3):
            for q in range(2):
                cx_s[i, r, :, cols[q]] = cov[q, (x + r) % 4, halves[i]].astype(BF16)
            cp = remote(cx_s.at[i, r], cx_r.at[i, r], cx_ss.at[i, r], cx_rs.at[i, r], to_x(r))
            cp.start()
            cx[i, r] = cp
            sent.append(cp)

    load_s.wait()
    factor = N * D / loss_share
    vgc = []

    def view_grad(i):
        rows = halves[i]
        for r in range(1, 4):
            cx[i, r].wait_recv()
        for q in range(2):
            at = cols[q]
            cov_prod = cov[q, x, rows]
            for r in range(1, 4):
                cov_prod = cov_prod + cx_r[i, r, :, at].astype(F32)
            values = xj[x, rows, at].astype(F32)
            centered = values - mean_j[:, at]
            invariance = 2.0 * inv_weight / (N * D) * (values - svb[rows, at].astype(F32))
            spread_term = -var_weight / D * hinge[:, at] * centered / ((N - 1) * deviation[:, at])
            cov_term = 4.0 * cov_weight / (D * (N - 1)) * (
                cov_prod / (N - 1) - centered * variance[:, at])
            vgs[i, :, at] = (factor * (invariance + spread_term + cov_term)).astype(BF16)
        cp = remote(vgs.at[i], vgp.at[i], vg_ss.at[i], vg_rs.at[i], partner)
        cp.start()
        vgc.append(cp)
        sent.append(cp)

    bk = []

    def back(i, r):
        at = (yl + r) % 4
        out = lax.dot_general(vgs[i], wb[at, 0], NT, preferred_element_type=F32)
        if r == 2:
            vgc[i].wait_recv()
        return out + lax.dot_general(vgp[i], wb[at, 1], NT, preferred_element_type=F32)

    def send_back(i):
        for r in (2, 1, 3):
            bk_s[i, r] = back(i, r).astype(BF16)
            cp = remote(bk_s.at[i, r], bk_r.at[i, r], bk_ss.at[i, r], bk_rs.at[i, r], to_yl(r))
            cp.start()
            bk.append(cp)
            sent.append(cp)

    for cp in load_w:
        cp.wait()
    for cp in lend_w:
        cp.wait_recv()
    for i in range(2):
        view_grad(i)
        send_back(i)
    load_p.wait()
    for i in range(2):
        vg_out[halves[i]] = vgs[i]
        keep[halves[i]] = back(i, 0)
    for cp in bk:
        cp.wait_recv()
    for i in range(2):
        total = keep[halves[i]]
        for r in range(1, 4):
            total = total + bk_r[i, r].astype(F32)
        pg_out[halves[i]] = jnp.where(pab[halves[i]] > 0, total, 0.0).astype(BF16)

    for cp in gj + gk[0][1:] + gk[1][1:] + s2 + [share_d] + lend_w + sent:
        cp.wait_send()

    @pl.when(jnp.logical_not(diagonal))
    def _():
        gk[0][0].wait_send()
        gk[1][0].wait_send()


def backward(first_view, second_view, weight, pre_act):
    dma = pltpu.SemaphoreType.DMA
    vmem = pltpu.VMEM
    return pl.pallas_call(
        kernel,
        out_shape=[jax.ShapeDtypeStruct((ROWS, COLS), BF16)] * 2,
        in_specs=[pl.BlockSpec(memory_space=pltpu.HBM)] * 4,
        out_specs=[pl.BlockSpec(memory_space=pltpu.VMEM)] * 2,
        scratch_shapes=[
            vmem((4, ROWS, COLS), BF16),
            vmem((2, 4, ROWS, HALF), BF16),
            vmem((4, ROWS, COLS), BF16),
            vmem((2, 2, 4, ROWS, HALF), BF16),
            vmem((ROWS, COLS), BF16),
            vmem((4, 2, COLS, COLS), BF16),
            vmem((ROWS, COLS), BF16),
            vmem((3, 1, COLS), F32),
            vmem((16, 3, 1, COLS), F32),
            vmem((16, COLS), F32),
            vmem((16, COLS), F32),
            vmem((48, COLS), BF16),
            vmem((2, 48, COLS), BF16),
            vmem((2, 8, UNIT, COLS), F32),
            vmem((2, 8, 2, UNIT, HALF), F32),
            vmem((2, 2, 4, 2, UNIT, HALF), BF16),
            vmem((2, 2, 4, 2, UNIT, HALF), BF16),
            vmem((2, 2, UNIT, HALF), BF16),
            vmem((2, 2, UNIT, HALF), BF16),
            vmem((2, 8, 2, UNIT, HALF), BF16),
            vmem((2, 4, ROWS, HALF), F32),
            vmem((2, 4, ROWS // 2, COLS), BF16),
            vmem((2, 4, ROWS // 2, COLS), BF16),
            vmem((2, ROWS // 2, COLS), BF16),
            vmem((2, ROWS // 2, COLS), BF16),
            vmem((2, 4, ROWS // 2, COLS), BF16),
            vmem((2, 4, ROWS // 2, COLS), BF16),
            vmem((ROWS, COLS), F32),
            dma((6,)),
            dma((4,)), dma((4,)), dma((2, 4)), dma((2, 4)), dma((16,)), dma((16,)), dma, dma,
            dma((2,)), dma((2,)), dma((2, 2, 4)), dma((2, 2, 4)), dma((2,)), dma((2,)),
            dma((2, 2, 4)), dma((2, 2, 4)),
            dma((2, 4)), dma((2, 4)), dma((2,)), dma((2,)), dma((2, 4)), dma((2, 4)),
            dma((4,)), dma((4,)), dma((4,)),
        ],
        compiler_params=pltpu.CompilerParams(
            collective_id=0, has_side_effects=True, vmem_limit_bytes=60 * 2**20),
        cost_estimate=pl.CostEstimate(flops=2700000000, bytes_accessed=5000000, transcendentals=0),
        name="vicreg_backward",
    )(first_view, second_view, weight.reshape(8, COLS, COLS), pre_act)


def store_kernel(a, b, a_out, b_out):
    a_out[...] = a[...]
    b_out[...] = b[...]


def on_device(*args):
    return pl.pallas_call(
        store_kernel,
        out_shape=[jax.ShapeDtypeStruct((ROWS, COLS), BF16)] * 2,
        in_specs=[pl.BlockSpec(memory_space=pltpu.VMEM)] * 2,
        out_specs=[pl.BlockSpec(memory_space=pltpu.VMEM)] * 2,
        compiler_params=pltpu.CompilerParams(vmem_limit_bytes=60 * 2**20),
        name="store",
    )(*backward(*args))


def solution(mesh):
    return jax.shard_map(
        on_device,
        mesh=mesh,
        in_specs=(P("pairs", "dims"), P("pairs", "dims"), P(None, "dims"), P("pairs", "dims")),
        out_specs=(P("pairs", "dims"), P("pairs", "dims")),
        check_vma=False,
    )
```

```python
import jax
import jax.numpy as jnp
from jax import lax
from jax.experimental import pallas as pl
from jax.experimental.pallas import tpu as pltpu
from jax.sharding import PartitionSpec as P

D = 4096
N = 8192
ROWS = 128
COLS = 512
UNIT = 64
HALF = 256
GROUP = 512

inv_weight = 25.0
var_weight = 25.0
cov_weight = 1.0
var_eps = 1e-05
loss_share = 32.0

F32 = jnp.float32
BF16 = jnp.bfloat16
NT = (((1,), (1,)), ((), ()))
TN = (((0,), (0,)), ((), ()))


def kernel(
    fv, sv, w, pa, vg_out, pg_out,
    xj, xk, pj, pk, svb, wb, pab,
    tot, st, dsj, dsk, dja, dkb, corr,
    cf, rs_s, rs_r, yh_s, yh_r, call,
    cov, cx_s, cx_r, vgs, vgp, bk_s, bk_r, keep,
    lsem,
    xj_ss, xj_rs, xk_ss, xk_rs, st_ss, st_rs, dk_ss, dk_rs,
    pk_ss, pk_rs, rsz_ss, rsz_rs, yh_ss, yh_rs, ag_ss, ag_rs,
    cx_ss, cx_rs, vg_ss, vg_rs, bk_ss, bk_rs, w_sem, w_ss, w_rs,
):
    p = lax.axis_index("pairs")
    d = lax.axis_index("dims")
    z, yh, x = p // 8, (p // 4) % 2, p % 4
    yl, c = d // 2, d % 2

    def dev(z_, yh_, x_, yl_, c_):
        return (z_ * 8 + yh_ * 4 + x_, yl_ * 2 + c_)

    def to_x(r):
        return dev(z, yh, (x + r) % 4, yl, c)

    def to_k(r):
        return dev(z, yh, yl, (x + r) % 4, c)

    def from_k(r):
        return dev(z, yh, (yl + 4 - r) % 4, x, c)

    def to_yl(r):
        return dev(z, yh, x, (yl + r) % 4, c)

    def to_z(r):
        return dev((z + r) % 8, yh, x, yl, c)

    partner = dev(z, yh, x, yl, 1 - c)
    across = dev(z, 1 - yh, x, yl, c)
    diagonal = x == yl

    def remote(src, dst, ss, rs, to):
        return pltpu.make_async_remote_copy(
            src_ref=src, dst_ref=dst, send_sem=ss, recv_sem=rs,
            device_id=to, device_id_type=pl.DeviceIdType.MESH)

    cols = (slice(0, HALF), slice(HALF, COLS))

    load_x = pltpu.make_async_copy(fv, xj.at[x], lsem.at[0])
    load_x.start()
    load_w = [
        pltpu.make_async_copy(w.at[i * 2 + c], wb.at[i, 0], w_sem.at[i]) for i in range(4)]
    load_s = pltpu.make_async_copy(sv, svb, lsem.at[2])
    load_p = pltpu.make_async_copy(pa, pab, lsem.at[3])
    load_k = [
        pltpu.make_async_copy(fv.at[:, cols[i]], xk.at[i, x], lsem.at[4 + i]) for i in range(2)]

    barrier = pltpu.get_barrier_semaphore()

    def greet(to):
        pl.semaphore_signal(barrier, inc=1, device_id=to, device_id_type=pl.DeviceIdType.MESH)

    count = 0
    for r in range(1, 8):
        greet(to_z(r))
        count += 1
    greet(across)
    count += 1
    for r in range(1, 4):
        greet(to_x(r))
        greet(to_k(r))
        greet(from_k(r))
        greet(to_yl(r))
        count += 4
    greet(partner)
    count += 1

    @pl.when(jnp.logical_not(diagonal))
    def _():
        greet(to_k(0))
        greet(from_k(0))

    @pl.when(diagonal)
    def _():
        for cp in load_k:
            cp.start()

    for cp in load_w:
        cp.start()
    load_s.start()
    load_p.start()
    load_x.wait()

    @pl.when(jnp.logical_not(diagonal))
    def _():
        pl.semaphore_wait(barrier, count + 2)

    @pl.when(diagonal)
    def _():
        pl.semaphore_wait(barrier, count)

    gj = [remote(xj.at[x], xj.at[x], xj_ss.at[r], xj_rs.at[r], to_x(r)) for r in range(1, 4)]
    gk = [[remote(xj.at[x, :, cols[i]], xk.at[i, x], xk_ss.at[i, r], xk_rs.at[i, r], to_k(r))
           for r in range(4)] for i in range(2)]

    def send_k(i):
        for cp in gk[i][1:]:
            cp.start()

        @pl.when(jnp.logical_not(diagonal))
        def _():
            gk[i][0].start()

    send_k(0)
    for cp in gj:
        cp.start()
    send_k(1)

    lend_w = [
        remote(w.at[i * 2 + 1 - c], wb.at[i, 1], w_ss.at[i], w_rs.at[i], partner) for i in range(4)]
    for cp in lend_w:
        cp.start()

    share = []

    def centre_k(i):
        for cp in gk[i][1:]:
            cp.wait_recv()

        @pl.when(jnp.logical_not(diagonal))
        def _():
            gk[i][0].wait_recv()

        @pl.when(diagonal)
        def _():
            load_k[i].wait()

        total = jnp.zeros((1, HALF), F32)
        for b in range(4):
            total = total + jnp.sum(xk[i, b].astype(F32), axis=0, keepdims=True)
        tot[2, :, cols[i]] = total
        for b in range(4):
            pk[0, i, b] = (xk[i, b].astype(F32) - total / GROUP).astype(BF16)
        cp = remote(pk.at[0, i], pk.at[1, i], pk_ss.at[i], pk_rs.at[i], partner)
        cp.start()
        share.append(cp)

    def centre_j():
        for cp in gj:
            cp.wait_recv()
        total = jnp.zeros((1, COLS), F32)
        for b in range(4):
            total = total + jnp.sum(xj[b].astype(F32), axis=0, keepdims=True)
        squares = jnp.zeros((1, COLS), F32)
        for b in range(4):
            centered = xj[b].astype(F32) - total / GROUP
            pj[b] = centered.astype(BF16)
            squares = squares + jnp.sum(centered * centered, axis=0, keepdims=True)
        tot[0] = total
        tot[1] = squares

    def block(i, h):
        prod = lax.dot_general(
            pj[...].reshape(GROUP, COLS), pk[h, i].reshape(GROUP, HALF), TN,
            preferred_element_type=F32)
        cf[i, :, h] = prod.reshape(8, UNIT, HALF)

    def along(way, hops):
        return dev((z + (hops if way == 0 else 8 - hops)) % 8, yh, x, yl, c)

    def unit(way, hops):
        return (z + (hops if way == 0 else 8 - hops)) % 8

    sent = []
    rs = {}

    def reduce_step(i, way, k):
        at = unit(way, k)
        if k == 4:
            held, land = rs_s.at[i, way, 3, way], rs_r.at[i, way, 3, way]
            rs_s[i, way, 3, way] = cf[i, at, way].astype(BF16)
        else:
            held, land = rs_s.at[i, way, k - 1], rs_r.at[i, way, k - 1]
            if k == 2:
                rs[i, way, 4].wait_recv()
                rs[i, way, 3].wait_recv()
            for h in range(2):
                val = cf[i, at, h]
                if k == 2 and h == way:
                    val = val + rs_r[i, way, 3, h].astype(F32)
                if k == 2:
                    val = val + rs_r[i, way, 2, h].astype(F32)
                rs_s[i, way, k - 1, h] = val.astype(BF16)
        cp = remote(held, land, rsz_ss.at[i, way, k - 1], rsz_rs.at[i, way, k - 1],
                    along(way, 1 if k % 2 else 2))
        cp.start()
        rs[i, way, k] = cp
        sent.append(cp)

    def reduce_all(i, *steps):
        for k in steps:
            for way in range(2):
                reduce_step(i, way, k)

    swap = {}

    def swap_out(i):
        for way in range(2):
            rs[i, way, 1].wait_recv()
            rs[i, way, 2].wait_recv()
        for h in range(2):
            mine = cf[i, z, h]
            for way in range(2):
                mine = mine + rs_r[i, way, 0, h].astype(F32) + rs_r[i, way, 1, h].astype(F32)
            cf[i, z, h] = mine
            yh_s[i, h] = mine.astype(BF16)
        cp = remote(yh_s.at[i], yh_r.at[i], yh_ss.at[i], yh_rs.at[i], across)
        cp.start()
        swap[i] = cp
        sent.append(cp)

    ag = {}

    def gather_step(i, way, k):
        if k == 4:
            ag[i, way, 2].wait_recv()
            held = call.at[i, unit(1 - way, 2), way]
        elif k == 3:
            held = call.at[i, unit(1 - way, 2)]
        else:
            held = call.at[i, z]
        cp = remote(held, held, ag_ss.at[i, way, k - 1], ag_rs.at[i, way, k - 1],
                    along(way, 1 if k % 2 else 2))
        cp.start()
        ag[i, way, k] = cp
        sent.append(cp)

    def gather_first(i):
        swap[i].wait_recv()
        for h in range(2):
            full = cf[i, z, h] + yh_r[i, h].astype(F32) + corr[h, z, :, cols[i]]
            call[i, z, h] = full.astype(BF16)
        gather_all(i, 2, 1)

    def gather_all(i, *steps):
        for k in steps:
            for way in range(2):
                gather_step(i, way, k)

    def gather_wait(i):
        for way in range(2):
            ag[i, way, 1].wait_recv()
            ag[i, way, 3].wait_recv()
            ag[i, way, 4].wait_recv()

    centre_k(0)
    centre_j()
    block(0, 0)
    share[0].wait_recv()
    block(0, 1)
    reduce_all(0, 4, 3, 1)
    centre_k(1)

    s2 = [remote(tot, st.at[r], st_ss.at[r], st_rs.at[r], to_z(r)) for r in range(1, 8)]
    for cp in s2:
        cp.start()
    block(1, 0)
    share[1].wait_recv()
    block(1, 1)
    reduce_all(1, 4, 3, 1)
    reduce_all(0, 2)
    st[0] = tot[...]
    for cp in s2:
        cp.wait_recv()
    s2.append(remote(st.at[pl.ds(0, 8)], st.at[pl.ds(8, 8)], st_ss.at[8], st_rs.at[8], across))
    s2[-1].start()
    reduce_all(1, 2)
    swap_out(0)
    swap_out(1)

    s2[-1].wait_recv()
    sums = st[0]
    for r in range(1, 16):
        sums = sums + st[r]
    mean_j, mean_k = sums[0] / N, sums[2] / N
    for r in range(16):
        dsj[r:r + 1, :] = st[r, 0] / GROUP - mean_j
        dsk[r:r + 1, :] = st[r, 2] / GROUP - mean_k
    gap_j, gap_k = dsj[...], dsk[...]
    variance = (sums[1] + GROUP * jnp.sum(gap_j * gap_j, axis=0, keepdims=True)) / (N - 1)
    deviation = jnp.sqrt(variance + var_eps)
    hinge = jnp.where(deviation < 1.0, 1.0, 0.0).astype(F32)

    def split(value):
        high = value.astype(BF16)
        return high, (value - high.astype(F32)).astype(BF16)

    high, low = split(GROUP * gap_j)
    dja[0:16], dja[16:32], dja[32:48] = high, high, low
    high, low = split(gap_k)
    dkb[0, 0:16], dkb[0, 16:32], dkb[0, 32:48] = high, low, high
    share_d = remote(dkb.at[0], dkb.at[1], dk_ss, dk_rs, partner)
    share_d.start()

    def correction(h):
        corr[h] = lax.dot_general(
            dja[...], dkb[h], TN, preferred_element_type=F32).reshape(8, UNIT, COLS)

    correction(0)
    share_d.wait_recv()
    correction(1)

    gather_first(0)
    gather_first(1)
    gather_all(0, 4, 3)

    for i in range(2):
        share[i].wait_send()
        for h in range(2):
            shift = dkb[h, 0:16].astype(F32)[0:1] + dkb[h, 16:32].astype(F32)[0:1]
            for b in range(4):
                pk[h, i, b] = (pk[h, i, b].astype(F32) + shift[:, cols[i]]).astype(BF16)
    gather_all(1, 4, 3)

    cx = {}

    def product(i, q):
        out = None
        for h in range(2):
            part = lax.dot_general(
                pk[h, i].reshape(GROUP, HALF), call[i, 4 * q:4 * q + 4, h].reshape(HALF, HALF), NT,
                preferred_element_type=F32)
            out = part if out is None else out + part
        return out.reshape(4, ROWS, HALF)

    gather_wait(0)
    for q in range(2):
        cov[q] = product(0, q)
    gather_wait(1)
    for q in range(2):
        cov[q] += product(1, q)
    halves = (slice(0, ROWS // 2), slice(ROWS // 2, ROWS))
    for i in range(2):
        for r in (2, 1, 3):
            for q in range(2):
                cx_s[i, r, :, cols[q]] = cov[q, (x + r) % 4, halves[i]].astype(BF16)
            cp = remote(cx_s.at[i, r], cx_r.at[i, r], cx_ss.at[i, r], cx_rs.at[i, r], to_x(r))
            cp.start()
            cx[i, r] = cp
            sent.append(cp)

    load_s.wait()
    factor = N * D / loss_share
    vgc = []

    def view_grad(i):
        rows = halves[i]
        for r in range(1, 4):
            cx[i, r].wait_recv()
        for q in range(2):
            at = cols[q]
            cov_prod = cov[q, x, rows]
            for r in range(1, 4):
                cov_prod = cov_prod + cx_r[i, r, :, at].astype(F32)
            values = xj[x, rows, at].astype(F32)
            centered = values - mean_j[:, at]
            invariance = 2.0 * inv_weight / (N * D) * (values - svb[rows, at].astype(F32))
            spread_term = -var_weight / D * hinge[:, at] * centered / ((N - 1) * deviation[:, at])
            cov_term = 4.0 * cov_weight / (D * (N - 1)) * (
                cov_prod / (N - 1) - centered * variance[:, at])
            vgs[i, :, at] = (factor * (invariance + spread_term + cov_term)).astype(BF16)
        cp = remote(vgs.at[i], vgp.at[i], vg_ss.at[i], vg_rs.at[i], partner)
        cp.start()
        vgc.append(cp)
        sent.append(cp)

    bk = []

    def back(i, r):
        at = (yl + r) % 4
        out = lax.dot_general(vgs[i], wb[at, 0], NT, preferred_element_type=F32)
        if r == 2:
            vgc[i].wait_recv()
        return out + lax.dot_general(vgp[i], wb[at, 1], NT, preferred_element_type=F32)

    def send_back(i):
        for r in (2, 1, 3):
            bk_s[i, r] = back(i, r).astype(BF16)
            cp = remote(bk_s.at[i, r], bk_r.at[i, r], bk_ss.at[i, r], bk_rs.at[i, r], to_yl(r))
            cp.start()
            bk.append(cp)
            sent.append(cp)

    for cp in load_w:
        cp.wait()
    for cp in lend_w:
        cp.wait_recv()
    for i in range(2):
        view_grad(i)
        send_back(i)
    load_p.wait()
    for i in range(2):
        vg_out[halves[i]] = vgs[i]
        keep[halves[i]] = back(i, 0)
    for cp in bk:
        cp.wait_recv()
    for i in range(2):
        total = keep[halves[i]]
        for r in range(1, 4):
            total = total + bk_r[i, r].astype(F32)
        pg_out[halves[i]] = jnp.where(pab[halves[i]] > 0, total, 0.0).astype(BF16)

    for cp in gj + gk[0][1:] + gk[1][1:] + s2 + [share_d] + lend_w + sent:
        cp.wait_send()

    @pl.when(jnp.logical_not(diagonal))
    def _():
        gk[0][0].wait_send()
        gk[1][0].wait_send()


def backward(first_view, second_view, weight, pre_act):
    dma = pltpu.SemaphoreType.DMA
    vmem = pltpu.VMEM
    return pl.pallas_call(
        kernel,
        out_shape=[jax.ShapeDtypeStruct((ROWS, COLS), BF16)] * 2,
        in_specs=[pl.BlockSpec(memory_space=pltpu.HBM)] * 4,
        out_specs=[pl.BlockSpec(memory_space=pltpu.VMEM)] * 2,
        scratch_shapes=[
            vmem((4, ROWS, COLS), BF16),
            vmem((2, 4, ROWS, HALF), BF16),
            vmem((4, ROWS, COLS), BF16),
            vmem((2, 2, 4, ROWS, HALF), BF16),
            vmem((ROWS, COLS), BF16),
            vmem((4, 2, COLS, COLS), BF16),
            vmem((ROWS, COLS), BF16),
            vmem((3, 1, COLS), F32),
            vmem((16, 3, 1, COLS), F32),
            vmem((16, COLS), F32),
            vmem((16, COLS), F32),
            vmem((48, COLS), BF16),
            vmem((2, 48, COLS), BF16),
            vmem((2, 8, UNIT, COLS), F32),
            vmem((2, 8, 2, UNIT, HALF), F32),
            vmem((2, 2, 4, 2, UNIT, HALF), BF16),
            vmem((2, 2, 4, 2, UNIT, HALF), BF16),
            vmem((2, 2, UNIT, HALF), BF16),
            vmem((2, 2, UNIT, HALF), BF16),
            vmem((2, 8, 2, UNIT, HALF), BF16),
            vmem((2, 4, ROWS, HALF), F32),
            vmem((2, 4, ROWS // 2, COLS), BF16),
            vmem((2, 4, ROWS // 2, COLS), BF16),
            vmem((2, ROWS // 2, COLS), BF16),
            vmem((2, ROWS // 2, COLS), BF16),
            vmem((2, 4, ROWS // 2, COLS), BF16),
            vmem((2, 4, ROWS // 2, COLS), BF16),
            vmem((ROWS, COLS), F32),
            dma((6,)),
            dma((4,)), dma((4,)), dma((2, 4)), dma((2, 4)), dma((16,)), dma((16,)), dma, dma,
            dma((2,)), dma((2,)), dma((2, 2, 4)), dma((2, 2, 4)), dma((2,)), dma((2,)),
            dma((2, 2, 4)), dma((2, 2, 4)),
            dma((2, 4)), dma((2, 4)), dma((2,)), dma((2,)), dma((2, 4)), dma((2, 4)),
            dma((4,)), dma((4,)), dma((4,)),
        ],
        compiler_params=pltpu.CompilerParams(
            collective_id=0, has_side_effects=True, vmem_limit_bytes=60 * 2**20),
        cost_estimate=pl.CostEstimate(flops=2700000000, bytes_accessed=5000000, transcendentals=0),
        name="vicreg_backward",
    )(first_view, second_view, weight.reshape(8, COLS, COLS), pre_act)


def store_kernel(a, b, a_out, b_out):
    a_out[...] = a[...]
    b_out[...] = b[...]


def on_device(*args):
    return pl.pallas_call(
        store_kernel,
        out_shape=[jax.ShapeDtypeStruct((ROWS, COLS), BF16)] * 2,
        in_specs=[pl.BlockSpec(memory_space=pltpu.VMEM)] * 2,
        out_specs=[pl.BlockSpec(memory_space=pltpu.VMEM)] * 2,
        compiler_params=pltpu.CompilerParams(vmem_limit_bytes=60 * 2**20),
        name="store",
    )(*backward(*args))


def solution(mesh):
    return jax.shard_map(
        on_device,
        mesh=mesh,
        in_specs=(P("pairs", "dims"), P("pairs", "dims"), P(None, "dims"), P("pairs", "dims")),
        out_specs=(P("pairs", "dims"), P("pairs", "dims")),
        check_vma=False,
    )
```

```python
import jax
import jax.numpy as jnp
from jax import lax
from jax.experimental import pallas as pl
from jax.experimental.pallas import tpu as pltpu
from jax.sharding import PartitionSpec as P

D = 4096
N = 8192
ROWS = 128
COLS = 512
UNIT = 64
HALF = 256
GROUP = 512

inv_weight = 25.0
var_weight = 25.0
cov_weight = 1.0
var_eps = 1e-05
loss_share = 32.0

F32 = jnp.float32
BF16 = jnp.bfloat16
NT = (((1,), (1,)), ((), ()))
TN = (((0,), (0,)), ((), ()))


def kernel(
    fv, sv, w, pa, vg_out, pg_out,
    xj, xk, pj, pk, svb, wb, pab,
    tot, st, dsj, dsk, dja, dkb, corr,
    cf, rs_s, rs_r, yh_s, yh_r, call,
    cov, cx_s, cx_r, vgs, vgp, bk_s, bk_r, keep,
    lsem,
    xj_ss, xj_rs, xk_ss, xk_rs, st_ss, st_rs, dk_ss, dk_rs,
    pk_ss, pk_rs, rsz_ss, rsz_rs, yh_ss, yh_rs, ag_ss, ag_rs,
    cx_ss, cx_rs, vg_ss, vg_rs, bk_ss, bk_rs, w_sem, w_ss, w_rs,
):
    p = lax.axis_index("pairs")
    d = lax.axis_index("dims")
    z, yh, x = p // 8, (p // 4) % 2, p % 4
    yl, c = d // 2, d % 2

    def dev(z_, yh_, x_, yl_, c_):
        return (z_ * 8 + yh_ * 4 + x_, yl_ * 2 + c_)

    def to_x(r):
        return dev(z, yh, (x + r) % 4, yl, c)

    def to_k(r):
        return dev(z, yh, yl, (x + r) % 4, c)

    def from_k(r):
        return dev(z, yh, (yl + 4 - r) % 4, x, c)

    def to_yl(r):
        return dev(z, yh, x, (yl + r) % 4, c)

    def to_z(r):
        return dev((z + r) % 8, yh, x, yl, c)

    partner = dev(z, yh, x, yl, 1 - c)
    across = dev(z, 1 - yh, x, yl, c)
    diagonal = x == yl

    def remote(src, dst, ss, rs, to):
        return pltpu.make_async_remote_copy(
            src_ref=src, dst_ref=dst, send_sem=ss, recv_sem=rs,
            device_id=to, device_id_type=pl.DeviceIdType.MESH)

    cols = (slice(0, HALF), slice(HALF, COLS))

    load_x = pltpu.make_async_copy(fv, xj.at[x], lsem.at[0])
    load_x.start()
    load_w = [
        pltpu.make_async_copy(w.at[i * 2 + c], wb.at[i, 0], w_sem.at[i]) for i in range(4)]
    load_s = pltpu.make_async_copy(sv, svb, lsem.at[2])
    load_p = pltpu.make_async_copy(pa, pab, lsem.at[3])
    load_k = [
        pltpu.make_async_copy(fv.at[:, cols[i]], xk.at[i, x], lsem.at[4 + i]) for i in range(2)]

    barrier = pltpu.get_barrier_semaphore()

    def greet(to):
        pl.semaphore_signal(barrier, inc=1, device_id=to, device_id_type=pl.DeviceIdType.MESH)

    @pl.when(jnp.logical_not(diagonal))
    def _():
        greet(to_k(0))
        greet(from_k(0))

    for r in range(1, 4):
        greet(to_k(r))
        greet(from_k(r))
    greet(across)
    for r in (4, 3, 5, 2, 6, 1, 7):
        greet(to_z(r))
    for r in range(1, 4):
        greet(to_yl(r))
        greet(to_x(r))
    greet(partner)
    count = 21

    @pl.when(diagonal)
    def _():
        for cp in load_k:
            cp.start()

    for cp in load_w:
        cp.start()
    load_s.start()
    load_p.start()
    load_x.wait()

    @pl.when(jnp.logical_not(diagonal))
    def _():
        pl.semaphore_wait(barrier, count + 2)

    @pl.when(diagonal)
    def _():
        pl.semaphore_wait(barrier, count)

    gj = [remote(xj.at[x], xj.at[x], xj_ss.at[r], xj_rs.at[r], to_x(r)) for r in range(1, 4)]
    gk = [[remote(xj.at[x, :, cols[i]], xk.at[i, x], xk_ss.at[i, r], xk_rs.at[i, r], to_k(r))
           for r in range(4)] for i in range(2)]

    def send_k(i):
        for cp in gk[i][1:]:
            cp.start()

        @pl.when(jnp.logical_not(diagonal))
        def _():
            gk[i][0].start()

    send_k(0)
    for cp in gj:
        cp.start()
    send_k(1)

    lend_w = [
        remote(w.at[i * 2 + 1 - c], wb.at[i, 1], w_ss.at[i], w_rs.at[i], partner) for i in range(4)]
    for cp in lend_w:
        cp.start()

    share = []

    def centre_k(i):
        for cp in gk[i][1:]:
            cp.wait_recv()

        @pl.when(jnp.logical_not(diagonal))
        def _():
            gk[i][0].wait_recv()

        @pl.when(diagonal)
        def _():
            load_k[i].wait()

        total = jnp.zeros((1, HALF), F32)
        for b in range(4):
            total = total + jnp.sum(xk[i, b].astype(F32), axis=0, keepdims=True)
        tot[2, :, cols[i]] = total
        for b in range(4):
            pk[0, i, b] = (xk[i, b].astype(F32) - total / GROUP).astype(BF16)
        cp = remote(pk.at[0, i], pk.at[1, i], pk_ss.at[i], pk_rs.at[i], partner)
        cp.start()
        share.append(cp)

    def centre_j():
        for cp in gj:
            cp.wait_recv()
        total = jnp.zeros((1, COLS), F32)
        for b in range(4):
            total = total + jnp.sum(xj[b].astype(F32), axis=0, keepdims=True)
        squares = jnp.zeros((1, COLS), F32)
        for b in range(4):
            centered = xj[b].astype(F32) - total / GROUP
            pj[b] = centered.astype(BF16)
            squares = squares + jnp.sum(centered * centered, axis=0, keepdims=True)
        tot[0] = total
        tot[1] = squares

    def block(i, h):
        prod = lax.dot_general(
            pj[...].reshape(GROUP, COLS), pk[h, i].reshape(GROUP, HALF), TN,
            preferred_element_type=F32)
        cf[i, :, h] = prod.reshape(8, UNIT, HALF)

    def along(way, hops):
        return dev((z + (hops if way == 0 else 8 - hops)) % 8, yh, x, yl, c)

    def unit(way, hops):
        return (z + (hops if way == 0 else 8 - hops)) % 8

    sent = []
    rs = {}

    def reduce_step(i, way, k):
        at = unit(way, k)
        if k == 4:
            held, land = rs_s.at[i, way, 3, way], rs_r.at[i, way, 3, way]
            rs_s[i, way, 3, way] = cf[i, at, way].astype(BF16)
        else:
            held, land = rs_s.at[i, way, k - 1], rs_r.at[i, way, k - 1]
            if k == 2:
                rs[i, way, 4].wait_recv()
                rs[i, way, 3].wait_recv()
            for h in range(2):
                val = cf[i, at, h]
                if k == 2 and h == way:
                    val = val + rs_r[i, way, 3, h].astype(F32)
                if k == 2:
                    val = val + rs_r[i, way, 2, h].astype(F32)
                rs_s[i, way, k - 1, h] = val.astype(BF16)
        cp = remote(held, land, rsz_ss.at[i, way, k - 1], rsz_rs.at[i, way, k - 1],
                    along(way, 1 if k % 2 else 2))
        cp.start()
        rs[i, way, k] = cp
        sent.append(cp)

    def reduce_all(i, *steps):
        for k in steps:
            for way in range(2):
                reduce_step(i, way, k)

    swap = {}

    def swap_out(i):
        for way in range(2):
            rs[i, way, 1].wait_recv()
            rs[i, way, 2].wait_recv()
        for h in range(2):
            mine = cf[i, z, h]
            for way in range(2):
                mine = mine + rs_r[i, way, 0, h].astype(F32) + rs_r[i, way, 1, h].astype(F32)
            cf[i, z, h] = mine
            yh_s[i, h] = mine.astype(BF16)
        cp = remote(yh_s.at[i], yh_r.at[i], yh_ss.at[i], yh_rs.at[i], across)
        cp.start()
        swap[i] = cp
        sent.append(cp)

    ag = {}

    def gather_step(i, way, k):
        if k == 4:
            ag[i, way, 2].wait_recv()
            held = call.at[i, unit(1 - way, 2), way]
        elif k == 3:
            held = call.at[i, unit(1 - way, 2)]
        else:
            held = call.at[i, z]
        cp = remote(held, held, ag_ss.at[i, way, k - 1], ag_rs.at[i, way, k - 1],
                    along(way, 1 if k % 2 else 2))
        cp.start()
        ag[i, way, k] = cp
        sent.append(cp)

    def gather_first(i):
        swap[i].wait_recv()
        for h in range(2):
            full = cf[i, z, h] + yh_r[i, h].astype(F32) + corr[h, z, :, cols[i]]
            call[i, z, h] = full.astype(BF16)
        gather_all(i, 2, 1)

    def gather_all(i, *steps):
        for k in steps:
            for way in range(2):
                gather_step(i, way, k)

    def gather_wait(i):
        for way in range(2):
            ag[i, way, 1].wait_recv()
            ag[i, way, 3].wait_recv()
            ag[i, way, 4].wait_recv()

    centre_k(0)
    centre_j()
    block(0, 0)
    share[0].wait_recv()
    block(0, 1)
    reduce_all(0, 4, 3, 1)
    centre_k(1)

    s2 = [remote(tot, st.at[r], st_ss.at[r], st_rs.at[r], to_z(r)) for r in range(1, 8)]
    for cp in s2:
        cp.start()
    block(1, 0)
    share[1].wait_recv()
    block(1, 1)
    reduce_all(1, 4, 3, 1)
    reduce_all(0, 2)
    st[0] = tot[...]
    for cp in s2:
        cp.wait_recv()
    s2.append(remote(st.at[pl.ds(0, 8)], st.at[pl.ds(8, 8)], st_ss.at[8], st_rs.at[8], across))
    s2[-1].start()
    reduce_all(1, 2)
    swap_out(0)
    swap_out(1)

    s2[-1].wait_recv()
    sums = st[0]
    for r in range(1, 16):
        sums = sums + st[r]
    mean_j, mean_k = sums[0] / N, sums[2] / N
    for r in range(16):
        dsj[r:r + 1, :] = st[r, 0] / GROUP - mean_j
        dsk[r:r + 1, :] = st[r, 2] / GROUP - mean_k
    gap_j, gap_k = dsj[...], dsk[...]
    variance = (sums[1] + GROUP * jnp.sum(gap_j * gap_j, axis=0, keepdims=True)) / (N - 1)
    deviation = jnp.sqrt(variance + var_eps)
    hinge = jnp.where(deviation < 1.0, 1.0, 0.0).astype(F32)

    def split(value):
        high = value.astype(BF16)
        return high, (value - high.astype(F32)).astype(BF16)

    high, low = split(GROUP * gap_j)
    dja[0:16], dja[16:32], dja[32:48] = high, high, low
    high, low = split(gap_k)
    dkb[0, 0:16], dkb[0, 16:32], dkb[0, 32:48] = high, low, high
    share_d = remote(dkb.at[0], dkb.at[1], dk_ss, dk_rs, partner)
    share_d.start()

    def correction(h):
        corr[h] = lax.dot_general(
            dja[...], dkb[h], TN, preferred_element_type=F32).reshape(8, UNIT, COLS)

    correction(0)
    share_d.wait_recv()
    correction(1)

    gather_first(0)
    gather_first(1)
    gather_all(0, 4, 3)

    for i in range(2):
        share[i].wait_send()
        for h in range(2):
            shift = dkb[h, 0:16].astype(F32)[0:1] + dkb[h, 16:32].astype(F32)[0:1]
            for b in range(4):
                pk[h, i, b] = (pk[h, i, b].astype(F32) + shift[:, cols[i]]).astype(BF16)
    gather_all(1, 4, 3)

    cx = {}

    def product(i, q):
        out = None
        for h in range(2):
            part = lax.dot_general(
                pk[h, i].reshape(GROUP, HALF), call[i, 4 * q:4 * q + 4, h].reshape(HALF, HALF), NT,
                preferred_element_type=F32)
            out = part if out is None else out + part
        return out.reshape(4, ROWS, HALF)

    gather_wait(0)
    for q in range(2):
        cov[q] = product(0, q)
    gather_wait(1)
    for q in range(2):
        cov[q] += product(1, q)
    halves = (slice(0, ROWS // 2), slice(ROWS // 2, ROWS))
    for i in range(2):
        for r in (2, 1, 3):
            for q in range(2):
                cx_s[i, r, :, cols[q]] = cov[q, (x + r) % 4, halves[i]].astype(BF16)
            cp = remote(cx_s.at[i, r], cx_r.at[i, r], cx_ss.at[i, r], cx_rs.at[i, r], to_x(r))
            cp.start()
            cx[i, r] = cp
            sent.append(cp)

    load_s.wait()
    factor = N * D / loss_share
    vgc = []

    def view_grad(i):
        rows = halves[i]
        for r in range(1, 4):
            cx[i, r].wait_recv()
        for q in range(2):
            at = cols[q]
            cov_prod = cov[q, x, rows]
            for r in range(1, 4):
                cov_prod = cov_prod + cx_r[i, r, :, at].astype(F32)
            values = xj[x, rows, at].astype(F32)
            centered = values - mean_j[:, at]
            invariance = 2.0 * inv_weight / (N * D) * (values - svb[rows, at].astype(F32))
            spread_term = -var_weight / D * hinge[:, at] * centered / ((N - 1) * deviation[:, at])
            cov_term = 4.0 * cov_weight / (D * (N - 1)) * (
                cov_prod / (N - 1) - centered * variance[:, at])
            vgs[i, :, at] = (factor * (invariance + spread_term + cov_term)).astype(BF16)
        cp = remote(vgs.at[i], vgp.at[i], vg_ss.at[i], vg_rs.at[i], partner)
        cp.start()
        vgc.append(cp)
        sent.append(cp)

    bk = []

    def back(i, r):
        at = (yl + r) % 4
        out = lax.dot_general(vgs[i], wb[at, 0], NT, preferred_element_type=F32)
        if r == 2:
            vgc[i].wait_recv()
        return out + lax.dot_general(vgp[i], wb[at, 1], NT, preferred_element_type=F32)

    def send_back(i):
        for r in (2, 1, 3):
            bk_s[i, r] = back(i, r).astype(BF16)
            cp = remote(bk_s.at[i, r], bk_r.at[i, r], bk_ss.at[i, r], bk_rs.at[i, r], to_yl(r))
            cp.start()
            bk.append(cp)
            sent.append(cp)

    for cp in load_w:
        cp.wait()
    for cp in lend_w:
        cp.wait_recv()
    for i in range(2):
        view_grad(i)
        send_back(i)
    load_p.wait()
    for i in range(2):
        vg_out[halves[i]] = vgs[i]
        keep[halves[i]] = back(i, 0)
    for cp in bk:
        cp.wait_recv()
    for i in range(2):
        total = keep[halves[i]]
        for r in range(1, 4):
            total = total + bk_r[i, r].astype(F32)
        pg_out[halves[i]] = jnp.where(pab[halves[i]] > 0, total, 0.0).astype(BF16)

    for cp in gj + gk[0][1:] + gk[1][1:] + s2 + [share_d] + lend_w + sent:
        cp.wait_send()

    @pl.when(jnp.logical_not(diagonal))
    def _():
        gk[0][0].wait_send()
        gk[1][0].wait_send()


def backward(first_view, second_view, weight, pre_act):
    dma = pltpu.SemaphoreType.DMA
    vmem = pltpu.VMEM
    return pl.pallas_call(
        kernel,
        out_shape=[jax.ShapeDtypeStruct((ROWS, COLS), BF16)] * 2,
        in_specs=[pl.BlockSpec(memory_space=pltpu.HBM)] * 4,
        out_specs=[pl.BlockSpec(memory_space=pltpu.VMEM)] * 2,
        scratch_shapes=[
            vmem((4, ROWS, COLS), BF16),
            vmem((2, 4, ROWS, HALF), BF16),
            vmem((4, ROWS, COLS), BF16),
            vmem((2, 2, 4, ROWS, HALF), BF16),
            vmem((ROWS, COLS), BF16),
            vmem((4, 2, COLS, COLS), BF16),
            vmem((ROWS, COLS), BF16),
            vmem((3, 1, COLS), F32),
            vmem((16, 3, 1, COLS), F32),
            vmem((16, COLS), F32),
            vmem((16, COLS), F32),
            vmem((48, COLS), BF16),
            vmem((2, 48, COLS), BF16),
            vmem((2, 8, UNIT, COLS), F32),
            vmem((2, 8, 2, UNIT, HALF), F32),
            vmem((2, 2, 4, 2, UNIT, HALF), BF16),
            vmem((2, 2, 4, 2, UNIT, HALF), BF16),
            vmem((2, 2, UNIT, HALF), BF16),
            vmem((2, 2, UNIT, HALF), BF16),
            vmem((2, 8, 2, UNIT, HALF), BF16),
            vmem((2, 4, ROWS, HALF), F32),
            vmem((2, 4, ROWS // 2, COLS), BF16),
            vmem((2, 4, ROWS // 2, COLS), BF16),
            vmem((2, ROWS // 2, COLS), BF16),
            vmem((2, ROWS // 2, COLS), BF16),
            vmem((2, 4, ROWS // 2, COLS), BF16),
            vmem((2, 4, ROWS // 2, COLS), BF16),
            vmem((ROWS, COLS), F32),
            dma((6,)),
            dma((4,)), dma((4,)), dma((2, 4)), dma((2, 4)), dma((16,)), dma((16,)), dma, dma,
            dma((2,)), dma((2,)), dma((2, 2, 4)), dma((2, 2, 4)), dma((2,)), dma((2,)),
            dma((2, 2, 4)), dma((2, 2, 4)),
            dma((2, 4)), dma((2, 4)), dma((2,)), dma((2,)), dma((2, 4)), dma((2, 4)),
            dma((4,)), dma((4,)), dma((4,)),
        ],
        compiler_params=pltpu.CompilerParams(
            collective_id=0, has_side_effects=True, vmem_limit_bytes=60 * 2**20),
        cost_estimate=pl.CostEstimate(flops=2700000000, bytes_accessed=5000000, transcendentals=0),
        name="vicreg_backward",
    )(first_view, second_view, weight.reshape(8, COLS, COLS), pre_act)


def store_kernel(a, b, a_out, b_out, held, sems):
    first = [pltpu.make_async_copy(src, held.at[i], sems.at[0, i]) for i, src in enumerate((a, b))]
    second = [pltpu.make_async_copy(held.at[i], dst, sems.at[1, i]) for i, dst in enumerate((a_out, b_out))]
    for cp in first:
        cp.start()
    for load, store in zip(first, second):
        load.wait()
        store.start()
    for cp in second:
        cp.wait()


def on_device(*args):
    return pl.pallas_call(
        store_kernel,
        out_shape=[jax.ShapeDtypeStruct((ROWS, COLS), BF16)] * 2,
        in_specs=[pl.BlockSpec(memory_space=pl.ANY)] * 2,
        out_specs=[pl.BlockSpec(memory_space=pl.ANY)] * 2,
        scratch_shapes=[pltpu.VMEM((2, ROWS, COLS), BF16), pltpu.SemaphoreType.DMA((2, 2))],
        compiler_params=pltpu.CompilerParams(vmem_limit_bytes=60 * 2**20),
        name="store",
    )(*backward(*args))


def solution(mesh):
    return jax.shard_map(
        on_device,
        mesh=mesh,
        in_specs=(P("pairs", "dims"), P("pairs", "dims"), P(None, "dims"), P("pairs", "dims")),
        out_specs=(P("pairs", "dims"), P("pairs", "dims")),
        check_vma=False,
    )
```
